256 devices in a mesh: dp: 32 (over x, z_hi, core), seq: 8 (over z_lo, y).
Axes of the slice: x: 4, y: 4, z: 8 (z_hi: 4, z_lo: 2; z = z_hi * 2 + z_lo), core: 2. Of those that a mesh axis runs over, the one named last changes fastest.
Arguments:
- query_rows: bfloat16 [32, 1024, 3072], P('dp', 'seq'), may hold values from -5 to 5
- key_rows: bfloat16 [32, 1024, 3072], P('dp', 'seq'), may hold values from -5 to 5
- value_rows: bfloat16 [32, 1024, 3072], P('dp', 'seq'), may hold values from -6 to 6
- query_tangent: bfloat16 [32, 1024, 3072], P('dp', 'seq'), may hold values from -6 to 6
- key_tangent: bfloat16 [32, 1024, 3072], P('dp', 'seq'), may hold values from -6 to 6
- value_tangent: bfloat16 [32, 1024, 3072], P('dp', 'seq'), may hold values from -6 to 6
- out_weight: bfloat16 [3072, 3072], P('dp'), may hold values from -0.109375 to 0.109375
- gate_scale: float32 [32, 3072], P('dp'), may hold values from -8 to 8
- gate_tangent: float32 [32, 3072], P('dp'), may hold values from -8 to 8
Outputs:
- gated_output: bfloat16 [32, 1024, 3072], P('dp', 'seq')
- output_tangent: bfloat16 [32, 1024, 3072], P('dp', 'seq')
The draws below stay inside these ranges and needn't reach their ends.
All inputs are finite; a program needn't handle non-finite values.
Results may differ from the reference program's by a relative error of at most 0.008.
Values may be sent and summed in bfloat16 or wider, within the bound.
No kernel may reach another device: no remote copies, remote signals or barrier semaphores. Data moves between devices by JAX's collectives and lax.ppermute only.
A program may use at most 128 MiB of HBM per device.

```python
import math
import jax
import jax.numpy as jnp
from jax import lax

HEAD_DIM = 128
HEADS = 24
DOUT = 3072
HD = 3072
SEQ = 1024
LATENTS = 32


def draw_query_rows(key, part):
    own_key = jax.random.fold_in(key, 1)
    result = jnp.clip(1.4 * jax.random.normal(own_key, (LATENTS, SEQ, HEADS, HEAD_DIM), jnp.float32), -5.0, 5.0)
    return result.reshape(LATENTS, SEQ, HEADS * HEAD_DIM).astype(jnp.bfloat16)


def draw_key_rows(key, part):
    own_key = jax.random.fold_in(key, 2)
    result = jnp.clip(1.4 * jax.random.normal(own_key, (LATENTS, SEQ, HEADS, HEAD_DIM), jnp.float32), -5.0, 5.0)
    return result.reshape(LATENTS, SEQ, HEADS * HEAD_DIM).astype(jnp.bfloat16)


def block_scale(key, dims, pieces, low, high):
    factor_of, own = 1.0, jax.random.fold_in(key, 6)
    for axis_at, shards_of in pieces:
        draws = jnp.exp(jax.random.uniform(jax.random.fold_in(own, axis_at), (shards_of,), jnp.float32, low / len(pieces), high / len(pieces)))
        factor_of = factor_of * jnp.repeat(draws, dims[axis_at] // shards_of).reshape([-1 if axis == axis_at else 1 for axis in range(len(dims))])
    return factor_of


def bell_draw(key, extent, scale, most, cuts=(), held_as=jnp.bfloat16):
    values = scale * jax.random.normal(key, extent, jnp.float32)
    if cuts:
        values = values * block_scale(key, extent, cuts, -0.22, 0.18)
    return jnp.clip(values, -most, most).astype(held_as)


def setup_inputs(seed: int = 0) -> dict:
    splits = jax.random.split(jax.random.key(seed), 10)
    return {
        "query_rows": draw_query_rows(jax.random.fold_in(splits[9], 71), 0),
        "key_rows": draw_key_rows(jax.random.fold_in(splits[9], 71), 0),
        "value_rows": bell_draw(splits[2], (LATENTS, SEQ, HD), 1.0, 6.0, ((0, 32), (1, 8))),
        "query_tangent": bell_draw(splits[3], (LATENTS, SEQ, HD), 1.0, 6.0, ((0, 32), (1, 8))),
        "key_tangent": bell_draw(splits[4], (LATENTS, SEQ, HD), 1.0, 6.0, ((0, 32), (1, 8))),
        "value_tangent": bell_draw(splits[5], (LATENTS, SEQ, HD), 1.0, 6.0, ((0, 32), (1, 8))),
        "out_weight": bell_draw(splits[6], (HD, DOUT), HD ** -0.5, 0.109375, ((0, 32),)),
        "gate_scale": bell_draw(splits[7], (LATENTS, DOUT), 2.0, 8.0, ((0, 32),), jnp.float32),
        "gate_tangent": bell_draw(splits[8], (LATENTS, DOUT), 2.0, 8.0, ((0, 32),), jnp.float32),
    }


def attend_head(operands):
    query_head, key_head, value_head, query_tan, key_tan, value_tan = operands
    factor = 1.0 / math.sqrt(HEAD_DIM)
    scores = jnp.dot(query_head, key_head.T, preferred_element_type=jnp.float32) * factor
    score_tangent = (jnp.dot(query_tan, key_head.T, preferred_element_type=jnp.float32) + jnp.dot(query_head, key_tan.T, preferred_element_type=jnp.float32)) * factor
    row_max = lax.optimization_barrier(jnp.max(scores, axis=1, keepdims=True))
    powers = jnp.exp(scores - row_max)
    weights = powers / lax.optimization_barrier(jnp.sum(powers, axis=1, keepdims=True))
    rounded_weights = weights.astype(jnp.bfloat16)
    tangent_mean = lax.optimization_barrier(jnp.sum(weights * score_tangent, axis=1, keepdims=True))
    weighted_tangent = (weights * score_tangent).astype(jnp.bfloat16)
    attended = jnp.dot(rounded_weights, value_head, preferred_element_type=jnp.float32)
    heads_tangent = jnp.dot(weighted_tangent, value_head, preferred_element_type=jnp.float32) + jnp.dot(rounded_weights, value_tan, preferred_element_type=jnp.float32) - tangent_mean * attended
    return (attended.astype(jnp.bfloat16), heads_tangent.astype(jnp.bfloat16))

def reference(query_rows, key_rows, value_rows, query_tangent, key_tangent, value_tangent, out_weight, gate_scale, gate_tangent):

    def split_heads(matrix):
        return jnp.transpose(matrix.reshape(SEQ, HEADS, HEAD_DIM), (1, 0, 2))

    def join_heads(tensor):
        return jnp.transpose(tensor, (1, 0, 2)).reshape(SEQ, HEADS * HEAD_DIM)

    def one_latent(operands):
        arrays = operands[:6]
        gate_row = operands[6]
        gate_tan_row = operands[7]
        stacked = tuple((split_heads(matrix) for matrix in arrays))
        heads_output, heads_tangent = lax.map(attend_head, stacked)
        projected = jnp.dot(join_heads(heads_output), out_weight, preferred_element_type=jnp.float32)
        projected_tangent = jnp.dot(join_heads(heads_tangent), out_weight, preferred_element_type=jnp.float32)
        gated = (gate_row[None, :] * projected).astype(jnp.bfloat16)
        tangent = (gate_tan_row[None, :] * projected + gate_row[None, :] * projected_tangent).astype(jnp.bfloat16)
        return (gated, tangent)
    gated_output, output_tangent = lax.map(one_latent, (query_rows, key_rows, value_rows, query_tangent, key_tangent, value_tangent, gate_scale, gate_tangent))
    return (gated_output, output_tangent)
```

```python
import math

import jax
import jax.numpy as jnp
from jax import lax
from jax.experimental import pallas as pl
from jax.experimental.pallas import tpu as pltpu
from jax.sharding import PartitionSpec as P

HEAD_DIM = 128
MIB = 1024 * 1024


def pack_kernel(*refs):
    out_ref = refs[-1]
    rows = refs[0].shape[1]
    for at, ref in enumerate(refs[:-1]):
        out_ref[0, at * rows : (at + 1) * rows, :] = ref[0]


def pack(arrays, pieces):
    _, rows, columns = arrays[0].shape
    width = columns // pieces
    return pl.pallas_call(
        pack_kernel,
        grid=(pieces,),
        in_specs=[pl.BlockSpec((1, rows, width), lambda s: (0, 0, s)) for _ in arrays],
        out_specs=pl.BlockSpec((1, len(arrays) * rows, width), lambda s: (s, 0, 0)),
        out_shape=jax.ShapeDtypeStruct((pieces, len(arrays) * rows, width), arrays[0].dtype),
        name="pack",
    )(*arrays)


def dot_rows(a, b):
    return lax.dot_general(a, b, (((1,), (1,)), ((), ())), preferred_element_type=jnp.float32)


def attend_kernel(x_ref, out_ref):
    pieces = x_ref.shape[0]
    rows = x_ref.shape[1] // 6
    tokens = pieces * rows
    factor = 1.0 / math.sqrt(HEAD_DIM)

    def whole(at):
        return x_ref[:, at * rows : (at + 1) * rows, :].reshape(tokens, HEAD_DIM)

    key, key_tan = whole(1), whole(4)
    keys = jnp.concatenate((key, key_tan), axis=1)
    value = whole(2)
    values = jnp.concatenate((value, whole(5)), axis=1)
    step = 2
    for block in range(0, pieces, step):
        many = slice(block, block + step)
        query = x_ref[many, 0:rows, :].reshape(step * rows, HEAD_DIM)
        query_tan = x_ref[many, 3 * rows : 4 * rows, :].reshape(step * rows, HEAD_DIM)
        scores = dot_rows(query, key)
        tangent = dot_rows(jnp.concatenate((query_tan, query), axis=1), keys)
        row_max = jnp.max(scores, axis=1, keepdims=True)
        powers = jnp.exp((scores - row_max) * factor)
        product = powers * tangent
        total = jnp.sum(powers, axis=1, keepdims=True)
        product_sum = jnp.sum(product, axis=1, keepdims=True)
        both = jnp.dot(
            powers.astype(jnp.bfloat16), values, preferred_element_type=jnp.float32
        )
        third = jnp.dot(
            product.astype(jnp.bfloat16), value, preferred_element_type=jnp.float32
        )
        inverse = 1.0 / total
        attended = both[:, :HEAD_DIM] * inverse
        mean = product_sum * (inverse * factor)
        heads_tan = third * (inverse * factor) + both[:, HEAD_DIM:] * inverse - mean * attended
        out_ref[many, 0:rows, :] = attended.astype(jnp.bfloat16).reshape(step, rows, HEAD_DIM)
        out_ref[many, rows : 2 * rows, :] = heads_tan.astype(jnp.bfloat16).reshape(
            step, rows, HEAD_DIM
        )


def attend(received):
    pieces, height, width = received.shape
    heads = width // HEAD_DIM
    rows = height // 6
    return pl.pallas_call(
        attend_kernel,
        grid=(heads,),
        in_specs=[pl.BlockSpec((pieces, height, HEAD_DIM), lambda h: (0, 0, h))],
        out_specs=pl.BlockSpec((pieces, 2 * rows, HEAD_DIM), lambda h: (0, 0, h)),
        out_shape=jax.ShapeDtypeStruct((pieces, 2 * rows, width), jnp.bfloat16),
        compiler_params=pltpu.CompilerParams(vmem_limit_bytes=48 * MIB),
        name="attend",
    )(received)


def project_kernel(x_ref, w_ref, scale_ref, tan_ref, gated_ref, out_tan_ref, all_ref):
    pieces, both_rows, width = x_ref.shape

    @pl.when(pl.program_id(0) == 0)
    def _():
        for piece in range(pieces):
            all_ref[:, piece * width : (piece + 1) * width] = x_ref[piece]

    rows = both_rows // 2
    projected = jnp.dot(all_ref[...], w_ref[...], preferred_element_type=jnp.float32)
    primal, tangent = projected[:rows], projected[rows:]
    scale = scale_ref[...]
    gated_ref[0] = (scale * primal).astype(jnp.bfloat16)
    out_tan_ref[0] = (tan_ref[...] * primal + scale * tangent).astype(jnp.bfloat16)


def project(x, weight, gate_scale, gate_tangent, block=512):
    pieces, both_rows, width = x.shape
    depth, columns = weight.shape
    rows = both_rows // 2
    out = jax.ShapeDtypeStruct((1, rows, columns), jnp.bfloat16)
    return pl.pallas_call(
        project_kernel,
        grid=(columns // block,),
        in_specs=[
            pl.BlockSpec((pieces, both_rows, width), lambda n: (0, 0, 0)),
            pl.BlockSpec((depth, block), lambda n: (0, n)),
            pl.BlockSpec((1, block), lambda n: (0, n)),
            pl.BlockSpec((1, block), lambda n: (0, n)),
        ],
        out_specs=[pl.BlockSpec((1, rows, block), lambda n: (0, 0, n))] * 2,
        out_shape=[out, out],
        scratch_shapes=[pltpu.VMEM((both_rows, depth), jnp.bfloat16)],
        compiler_params=pltpu.CompilerParams(vmem_limit_bytes=48 * MIB),
        name="project",
    )(x, weight, gate_scale, gate_tangent)


def on_device(
    query_rows,
    key_rows,
    value_rows,
    query_tangent,
    key_tangent,
    value_tangent,
    out_weight,
    gate_scale,
    gate_tangent,
):
    pieces = lax.axis_size("seq")
    weight = lax.all_gather(out_weight, "dp", axis=0, tiled=True)
    sent = pack(
        (query_rows, key_rows, value_rows, query_tangent, key_tangent, value_tangent), pieces
    )
    received = lax.all_to_all(sent, "seq", 0, 0, tiled=True)
    results = lax.all_to_all(attend(received), "seq", 0, 0, tiled=True)
    gated, tangent = project(results, weight, gate_scale, gate_tangent)
    return (gated, tangent)


def solution(mesh):
    rows = P("dp", "seq", None)
    placed = (rows,) * 6 + (P("dp", None),) * 3
    return jax.shard_map(
        on_device,
        mesh=mesh,
        in_specs=placed,
        out_specs=(rows, rows),
        check_vma=False,
    )
```

```python
import math

import jax
import jax.numpy as jnp
from jax import lax
from jax.experimental import pallas as pl
from jax.experimental.pallas import tpu as pltpu
from jax.sharding import PartitionSpec as P

HEAD_DIM = 128
MIB = 1024 * 1024


def flat(x, z, core, y):
    dp = (x % 4) * 8 + ((z % 8) // 2) * 2 + core
    return dp * 8 + (z % 2) * 4 + y % 4


def moves(target):
    return [
        (flat(x, z, core, y), flat(*target(x, z, core, y)))
        for x in range(4)
        for z in range(8)
        for core in range(2)
        for y in range(4)
    ]


AXES = ("dp", "seq")
NEXT_X = moves(lambda x, z, core, y: (x + 1, z, core, y))
LAST_X = moves(lambda x, z, core, y: (x - 1, z, core, y))
OUTER_Z = moves(lambda x, z, core, y: (x, z + 1 if z % 2 else z - 1, core, y))
INNER_Z = moves(lambda x, z, core, y: (x, z - 1 if z % 2 else z + 1, core, y))
OTHER_CORE = moves(lambda x, z, core, y: (x, z, 1 - core, y))
OFFSETS = [(a, b) for a in range(2) for b in range(4)]


def seq_moves(offset, back=False):
    a, b = offset
    there = [(z * 4 + y, (z + a) % 2 * 4 + (y + b) % 4) for z in range(2) for y in range(4)]
    return [(q, p) for p, q in there] if back else there


def shifted(seq, offset):
    a, b = offset
    return (seq // 4 + a) % 2 * 4 + (seq % 4 + b) % 4


def pack_kernel(group_ref, *refs):
    sources, out_ref, sem = refs[:-2], refs[-2], refs[-1]
    rows, width = out_ref.shape[0] // len(sources), out_ref.shape[1]
    columns = pl.ds(pl.multiple_of(group_ref[0] * width, width), width)
    for at, ref in enumerate(sources):
        pltpu.make_async_copy(
            ref.at[0, :, columns], out_ref.at[pl.ds(at * rows, rows), :], sem
        ).start()
    pltpu.make_async_copy(out_ref, out_ref, sem).wait()


def pack(arrays, group, pieces):
    _, rows, columns = arrays[0].shape
    height, width = len(arrays) * rows, columns // pieces
    anywhere = pl.BlockSpec(memory_space=pltpu.HBM)
    return pl.pallas_call(
        pack_kernel,
        in_specs=[pl.BlockSpec(memory_space=pltpu.SMEM)] + [anywhere] * len(arrays),
        out_specs=anywhere,
        out_shape=jax.ShapeDtypeStruct((height, width), arrays[0].dtype),
        scratch_shapes=[pltpu.SemaphoreType.DMA],
        cost_estimate=pl.CostEstimate(
            flops=0, bytes_accessed=4 * height * width, transcendentals=0
        ),
        name="pack",
    )(group.reshape(1), *arrays)


def dot_rows(a, b):
    return lax.dot_general(a, b, (((1,), (1,)), ((), ())), preferred_element_type=jnp.float32)


def attend_kernel(*refs):
    pieces = len(refs) // 2
    ins, outs = refs[:pieces], refs[pieces:]
    rows = ins[0].shape[0] // 6
    factor = 1.0 / math.sqrt(HEAD_DIM)

    def part(at, which):
        return jnp.concatenate([ins[p][at * rows : (at + 1) * rows, :] for p in which], axis=0)

    every = range(pieces)
    key, value = part(1, every), part(2, every)
    keys = jnp.concatenate((key, part(4, every)), axis=1)
    values = jnp.concatenate((value, part(5, every)), axis=1)
    step = 2
    for block in range(0, pieces, step):
        which = range(block, block + step)
        query, query_tan = part(0, which), part(3, which)
        scores = dot_rows(query, key)
        tangent = dot_rows(jnp.concatenate((query_tan, query), axis=1), keys)
        row_max = jnp.max(scores, axis=1, keepdims=True)
        powers = jnp.exp((scores - row_max) * factor)
        product = powers * tangent
        total = jnp.sum(powers, axis=1, keepdims=True)
        product_sum = jnp.sum(product, axis=1, keepdims=True)
        both = jnp.dot(powers.astype(jnp.bfloat16), values, preferred_element_type=jnp.float32)
        third = jnp.dot(product.astype(jnp.bfloat16), value, preferred_element_type=jnp.float32)
        inverse = 1.0 / total
        attended = both[:, :HEAD_DIM] * inverse
        mean = product_sum * (inverse * factor)
        heads_tan = third * (inverse * factor) + both[:, HEAD_DIM:] * inverse - mean * attended
        attended = attended.astype(jnp.bfloat16)
        heads_tan = heads_tan.astype(jnp.bfloat16)
        for at, p in enumerate(which):
            outs[p][0:rows, :] = attended[at * rows : (at + 1) * rows]
            outs[p][rows : 2 * rows, :] = heads_tan[at * rows : (at + 1) * rows]


def attend(received):
    height, width = received[0].shape
    heads = width // HEAD_DIM
    rows = height // 6
    tokens = rows * len(received)
    out = jax.ShapeDtypeStruct((2 * rows, width), jnp.bfloat16)
    return pl.pallas_call(
        attend_kernel,
        grid=(heads,),
        in_specs=[pl.BlockSpec((height, HEAD_DIM), lambda h: (0, h))] * len(received),
        out_specs=[pl.BlockSpec((2 * rows, HEAD_DIM), lambda h: (0, h))] * len(received),
        out_shape=[out] * len(received),
        compiler_params=pltpu.CompilerParams(vmem_limit_bytes=60 * MIB),
        cost_estimate=pl.CostEstimate(
            flops=heads * 12 * tokens * tokens * HEAD_DIM,
            bytes_accessed=len(received) * (height + 2 * rows) * width * 2,
            transcendentals=heads * tokens * tokens,
        ),
        name="attend",
    )(*received)


BLOCK = 512


def project_kernel(shard_ref, group_ref, *refs):
    shards, pieces = shard_ref.shape[0], group_ref.shape[0]
    weights, refs = refs[:shards], refs[shards:]
    parts, refs = refs[:pieces], refs[pieces:]
    scale_ref, tan_ref, gated_ref, out_tan_ref, all_ref, held_ref, sem = refs
    depth = weights[0].shape[0]
    blocks = held_ref.shape[0]
    for n in range(blocks):
        for at, weight in enumerate(weights):
            place = pl.ds(pl.multiple_of(shard_ref[at] * depth, depth), depth)
            pltpu.make_async_copy(
                weight.at[:, n * BLOCK : (n + 1) * BLOCK], held_ref.at[n, place, :], sem.at[n]
            ).start()
    width = parts[0].shape[1]
    for at, part in enumerate(parts):
        all_ref[:, pl.ds(pl.multiple_of(group_ref[at] * width, width), width)] = part[...]
    rows = gated_ref.shape[1]
    for n in range(blocks):
        pltpu.make_async_copy(held_ref.at[n], held_ref.at[n], sem.at[n]).wait()
        projected = jnp.dot(all_ref[...], held_ref[n], preferred_element_type=jnp.float32)
        primal, tangent = projected[:rows], projected[rows:]
        columns = slice(n * BLOCK, (n + 1) * BLOCK)
        scale = scale_ref[:, columns]
        gated_ref[0, :, columns] = (scale * primal).astype(jnp.bfloat16)
        out_tan_ref[0, :, columns] = (tan_ref[:, columns] * primal + scale * tangent).astype(
            jnp.bfloat16
        )


def project(weights, shard_at, parts, group_at, gate_scale, gate_tangent):
    depth, columns = weights[0].shape
    both_rows, width = parts[0].shape
    rows, total = both_rows // 2, depth * len(weights)
    out = jax.ShapeDtypeStruct((1, rows, columns), jnp.bfloat16)
    in_smem = pl.BlockSpec(memory_space=pltpu.SMEM)
    in_vmem = pl.BlockSpec(memory_space=pltpu.VMEM)
    return pl.pallas_call(
        project_kernel,
        in_specs=[in_smem] * 2
        + [pl.BlockSpec(memory_space=pltpu.HBM)] * len(weights)
        + [in_vmem] * (len(parts) + 2),
        out_specs=[in_vmem] * 2,
        out_shape=[out, out],
        scratch_shapes=[
            pltpu.VMEM((both_rows, total), jnp.bfloat16),
            pltpu.VMEM((columns // BLOCK, total, BLOCK), jnp.bfloat16),
            pltpu.SemaphoreType.DMA((columns // BLOCK,)),
        ],
        compiler_params=pltpu.CompilerParams(vmem_limit_bytes=60 * MIB),
        cost_estimate=pl.CostEstimate(
            flops=2 * both_rows * total * columns,
            bytes_accessed=2 * total * columns,
            transcendentals=0,
        ),
        name="project",
    )(shard_at, group_at, *weights, *parts, gate_scale, gate_tangent)


def send(value, moves_of, *after, axes=AXES):
    if after:
        value = lax.optimization_barrier((value,) + after)[0]
    return lax.ppermute(value, axes, moves_of)


def on_device(
    query_rows,
    key_rows,
    value_rows,
    query_tangent,
    key_tangent,
    value_tangent,
    out_weight,
    gate_scale,
    gate_tangent,
):
    dp, seq = lax.axis_index("dp"), lax.axis_index("seq")
    groups = [shifted(seq, offset).astype(jnp.int32) for offset in OFFSETS]
    arrays = (query_rows, key_rows, value_rows, query_tangent, key_tangent, value_tangent)

    def forward(offset, *after):
        a, b = offset
        sent = pack(arrays, groups[a * 4 + b], len(OFFSETS))
        return send(sent, seq_moves(offset), *after, axes="seq")

    z, before, later, far, tokens = {0: out_weight}, {}, {}, {}, {}
    z[1] = send(z[0], OUTER_Z)
    before[0] = send(z[0], NEXT_X)
    later[0] = send(z[0], LAST_X)
    tokens[0, 1] = forward((0, 1))
    tokens[1, 3] = forward((1, 3))

    z[2] = send(z[1], INNER_Z)
    far[0] = send(before[0], NEXT_X)
    later[1] = send(z[1], LAST_X, later[0])
    tokens[0, 2] = forward((0, 2), tokens[0, 1])

    z[3] = send(z[2], OUTER_Z)
    before[1] = send(z[1], NEXT_X, far[0])
    far[1] = send(later[1], LAST_X)
    tokens[1, 1] = forward((1, 1), tokens[1, 3])
    tokens[0, 3] = forward((0, 3), tokens[0, 2])

    before[2] = send(z[2], NEXT_X, before[1])
    later[2] = send(z[2], LAST_X, far[1])
    tokens[1, 2] = forward((1, 2), tokens[1, 1])
    tokens[1, 0] = forward((1, 0), tokens[0, 3])

    far[2] = send(before[2], NEXT_X)
    later[3] = send(z[3], LAST_X, later[2])
    before[3] = send(z[3], NEXT_X, far[2])
    far[3] = send(later[3], LAST_X)

    tokens[0, 0] = pack(arrays, groups[0], len(OFFSETS))
    results = attend([tokens[offset] for offset in OFFSETS])

    x, z_pair, core, right = dp // 8, dp // 2 % 4, dp % 2, seq // 4
    toward = 2 * right - 1
    pairs = (0, toward, -toward, 2)
    freed = (before[1], before[2], far[2], before[3])
    weights, places = [], []
    for at in range(4):
        for block, steps in ((z[at], 0), (before[at], -1), (later[at], 1), (far[at], 2)):
            place = (x + steps) % 4 * 8 + (z_pair + pairs[at]) % 4 * 2
            weights.append(block)
            places.append(place + core)
            weights.append(send(block, OTHER_CORE, freed[at]))
            places.append(place + 1 - core)
    parts = []
    for offset, result in zip(OFFSETS, results):
        parts.append(
            result
            if offset == (0, 0)
            else send(result, seq_moves(offset, back=True), axes="seq")
        )
    shard_at = jnp.stack(places).astype(jnp.int32)
    gated, tangent = project(
        weights, shard_at, parts, jnp.stack(groups), gate_scale, gate_tangent
    )
    return (gated, tangent)


def solution(mesh):
    rows = P("dp", "seq", None)
    placed = (rows,) * 6 + (P("dp", None),) * 3
    return jax.shard_map(
        on_device,
        mesh=mesh,
        in_specs=placed,
        out_specs=(rows, rows),
        check_vma=False,
    )
```

```python
import math

import jax
import jax.numpy as jnp
from jax import lax
from jax.experimental import pallas as pl
from jax.experimental.pallas import tpu as pltpu
from jax.sharding import PartitionSpec as P

HEAD_DIM = 128
MIB = 1024 * 1024


def flat(x, z, core, y):
    dp = (x % 4) * 8 + ((z % 8) // 2) * 2 + core
    return dp * 8 + (z % 2) * 4 + y % 4


def moves(target):
    return [
        (flat(x, z, core, y), flat(*target(x, z, core, y)))
        for x in range(4)
        for z in range(8)
        for core in range(2)
        for y in range(4)
    ]


AXES = ("dp", "seq")
NEXT_X = moves(lambda x, z, core, y: (x + 1, z, core, y))
LAST_X = moves(lambda x, z, core, y: (x - 1, z, core, y))
OUTER_Z = moves(lambda x, z, core, y: (x, z + 1 if z % 2 else z - 1, core, y))
INNER_Z = moves(lambda x, z, core, y: (x, z - 1 if z % 2 else z + 1, core, y))
OTHER_CORE = moves(lambda x, z, core, y: (x, z, 1 - core, y))
OFFSETS = [(a, b) for a in range(2) for b in range(4)]


def seq_moves(offset, back=False):
    a, b = offset
    there = [(z * 4 + y, (z + a) % 2 * 4 + (y + b) % 4) for z in range(2) for y in range(4)]
    return [(q, p) for p, q in there] if back else there


def shifted(seq, offset):
    a, b = offset
    return (seq // 4 + a) % 2 * 4 + (seq % 4 + b) % 4


def pack_kernel(group_ref, *refs):
    pieces = group_ref.shape[0]
    ins, outs = refs[:-pieces], refs[-pieces:]
    width = outs[0].shape[2]
    for piece, out_ref in enumerate(outs):
        columns = pl.ds(pl.multiple_of(group_ref[piece] * width, width), width)
        for at, ref in enumerate(ins):
            out_ref[at] = ref[0, :, columns]


def pack(arrays, groups, block=32):
    _, rows, columns = arrays[0].shape
    pieces, width = groups.shape[0], columns // groups.shape[0]
    out = jax.ShapeDtypeStruct((len(arrays), rows, width), arrays[0].dtype)
    return pl.pallas_call(
        pack_kernel,
        grid_spec=pltpu.PrefetchScalarGridSpec(
            num_scalar_prefetch=1,
            grid=(rows // block,),
            in_specs=[
                pl.BlockSpec((1, block, columns), lambda i, group: (0, i, 0)) for _ in arrays
            ],
            out_specs=[pl.BlockSpec((len(arrays), block, width), lambda i, group: (0, i, 0))]
            * pieces,
        ),
        out_shape=[out] * pieces,
        cost_estimate=pl.CostEstimate(
            flops=0, bytes_accessed=4 * len(arrays) * rows * columns, transcendentals=0
        ),
        name="pack",
    )(groups, *arrays)


def dot_rows(a, b):
    return lax.dot_general(a, b, (((1,), (1,)), ((), ())), preferred_element_type=jnp.float32)


def attend_kernel(*refs):
    pieces = len(refs) // 2
    ins, outs = refs[:pieces], refs[pieces:]
    rows = ins[0].shape[1]
    factor = 1.0 / math.sqrt(HEAD_DIM)

    def part(at, which):
        return jnp.concatenate([ins[p][at] for p in which], axis=0)

    every = range(pieces)
    key, value = part(1, every), part(2, every)
    keys = jnp.concatenate((key, part(4, every)), axis=1)
    values = jnp.concatenate((value, part(5, every)), axis=1)
    step = 2
    for block in range(0, pieces, step):
        which = range(block, block + step)
        query, query_tan = part(0, which), part(3, which)
        scores = dot_rows(query, key)
        tangent = dot_rows(jnp.concatenate((query_tan, query), axis=1), keys)
        row_max = jnp.max(scores, axis=1, keepdims=True)
        powers = jnp.exp((scores - row_max) * factor)
        product = powers * tangent
        total = jnp.sum(powers, axis=1, keepdims=True)
        product_sum = jnp.sum(product, axis=1, keepdims=True)
        both = jnp.dot(powers.astype(jnp.bfloat16), values, preferred_element_type=jnp.float32)
        third = jnp.dot(product.astype(jnp.bfloat16), value, preferred_element_type=jnp.float32)
        inverse = 1.0 / total
        attended = both[:, :HEAD_DIM] * inverse
        mean = product_sum * (inverse * factor)
        heads_tan = third * (inverse * factor) + both[:, HEAD_DIM:] * inverse - mean * attended
        attended = attended.astype(jnp.bfloat16)
        heads_tan = heads_tan.astype(jnp.bfloat16)
        for at, p in enumerate(which):
            outs[p][0:rows, :] = attended[at * rows : (at + 1) * rows]
            outs[p][rows : 2 * rows, :] = heads_tan[at * rows : (at + 1) * rows]


def attend(received):
    count, rows, width = received[0].shape
    heads = width // HEAD_DIM
    tokens = rows * len(received)
    out = jax.ShapeDtypeStruct((2 * rows, width), jnp.bfloat16)
    return pl.pallas_call(
        attend_kernel,
        grid=(heads,),
        in_specs=[pl.BlockSpec((count, rows, HEAD_DIM), lambda h: (0, 0, h))] * len(received),
        out_specs=[pl.BlockSpec((2 * rows, HEAD_DIM), lambda h: (0, h))] * len(received),
        out_shape=[out] * len(received),
        compiler_params=pltpu.CompilerParams(vmem_limit_bytes=60 * MIB),
        cost_estimate=pl.CostEstimate(
            flops=heads * 12 * tokens * tokens * HEAD_DIM,
            bytes_accessed=len(received) * (count + 2) * rows * width * 2,
            transcendentals=heads * tokens * tokens,
        ),
        name="attend",
    )(*received)


BLOCK = 512


def project_kernel(shard_ref, group_ref, *refs):
    shards, pieces = shard_ref.shape[0], group_ref.shape[0]
    weights, refs = refs[:shards], refs[shards:]
    parts, refs = refs[:pieces], refs[pieces:]
    scale_ref, tan_ref, gated_ref, out_tan_ref, all_ref, held_ref, sem = refs
    depth = weights[0].shape[0]
    blocks = held_ref.shape[0]
    for n in range(blocks):
        for at, weight in enumerate(weights):
            place = pl.ds(pl.multiple_of(shard_ref[at] * depth, depth), depth)
            pltpu.make_async_copy(
                weight.at[:, n * BLOCK : (n + 1) * BLOCK], held_ref.at[n, place, :], sem.at[n]
            ).start()
    width = parts[0].shape[1]
    for at, part in enumerate(parts):
        all_ref[:, pl.ds(pl.multiple_of(group_ref[at] * width, width), width)] = part[...]
    rows = gated_ref.shape[1]
    for n in range(blocks):
        pltpu.make_async_copy(held_ref.at[n], held_ref.at[n], sem.at[n]).wait()
        projected = jnp.dot(all_ref[...], held_ref[n], preferred_element_type=jnp.float32)
        primal, tangent = projected[:rows], projected[rows:]
        columns = slice(n * BLOCK, (n + 1) * BLOCK)
        scale = scale_ref[:, columns]
        gated_ref[0, :, columns] = (scale * primal).astype(jnp.bfloat16)
        out_tan_ref[0, :, columns] = (tan_ref[:, columns] * primal + scale * tangent).astype(
            jnp.bfloat16
        )


def project(weights, shard_at, parts, group_at, gate_scale, gate_tangent):
    depth, columns = weights[0].shape
    both_rows, width = parts[0].shape
    rows, total = both_rows // 2, depth * len(weights)
    out = jax.ShapeDtypeStruct((1, rows, columns), jnp.bfloat16)
    in_smem = pl.BlockSpec(memory_space=pltpu.SMEM)
    in_vmem = pl.BlockSpec(memory_space=pltpu.VMEM)
    return pl.pallas_call(
        project_kernel,
        in_specs=[in_smem] * 2
        + [pl.BlockSpec(memory_space=pltpu.HBM)] * len(weights)
        + [in_vmem] * (len(parts) + 2),
        out_specs=[in_vmem] * 2,
        out_shape=[out, out],
        scratch_shapes=[
            pltpu.VMEM((both_rows, total), jnp.bfloat16),
            pltpu.VMEM((columns // BLOCK, total, BLOCK), jnp.bfloat16),
            pltpu.SemaphoreType.DMA((columns // BLOCK,)),
        ],
        compiler_params=pltpu.CompilerParams(vmem_limit_bytes=60 * MIB),
        cost_estimate=pl.CostEstimate(
            flops=2 * both_rows * total * columns,
            bytes_accessed=2 * total * columns,
            transcendentals=0,
        ),
        name="project",
    )(shard_at, group_at, *weights, *parts, gate_scale, gate_tangent)


def send(value, moves_of, *after, axes=AXES):
    if after:
        value = lax.optimization_barrier((value,) + after)[0]
    return lax.ppermute(value, axes, moves_of)


def on_device(
    query_rows,
    key_rows,
    value_rows,
    query_tangent,
    key_tangent,
    value_tangent,
    out_weight,
    gate_scale,
    gate_tangent,
):
    dp, seq = lax.axis_index("dp"), lax.axis_index("seq")
    groups = jnp.stack([shifted(seq, offset) for offset in OFFSETS]).astype(jnp.int32)
    arrays = (query_rows, key_rows, value_rows, query_tangent, key_tangent, value_tangent)

    packed = dict(zip(OFFSETS, pack(arrays, groups)))

    def forward(offset, *after):
        return send(packed[offset], seq_moves(offset), *after, axes="seq")

    z, before, later, far, tokens = {0: out_weight}, {}, {}, {}, {}
    z[1] = send(z[0], OUTER_Z)
    before[0] = send(z[0], NEXT_X)
    later[0] = send(z[0], LAST_X)
    tokens[0, 1] = forward((0, 1))
    tokens[1, 3] = forward((1, 3))

    z[2] = send(z[1], INNER_Z)
    far[0] = send(before[0], NEXT_X)
    later[1] = send(z[1], LAST_X, later[0])
    tokens[0, 2] = forward((0, 2), tokens[0, 1])

    z[3] = send(z[2], OUTER_Z)
    before[1] = send(z[1], NEXT_X, far[0])
    far[1] = send(later[1], LAST_X)
    tokens[1, 1] = forward((1, 1), tokens[1, 3])
    tokens[0, 3] = forward((0, 3), tokens[0, 2])

    before[2] = send(z[2], NEXT_X, before[1])
    later[2] = send(z[2], LAST_X, far[1])
    tokens[1, 2] = forward((1, 2), tokens[1, 1])
    tokens[1, 0] = forward((1, 0), tokens[0, 3])

    far[2] = send(before[2], NEXT_X)
    later[3] = send(z[3], LAST_X, later[2])
    before[3] = send(z[3], NEXT_X, far[2])
    far[3] = send(later[3], LAST_X)

    tokens[0, 0] = packed[0, 0]
    results = attend([tokens[offset] for offset in OFFSETS])

    x, z_pair, core, right = dp // 8, dp // 2 % 4, dp % 2, seq // 4
    toward = 2 * right - 1
    pairs = (0, toward, -toward, 2)
    freed = (before[1], before[2], far[2], before[3])
    weights, places = [], []
    for at in range(4):
        for block, steps in ((z[at], 0), (before[at], -1), (later[at], 1), (far[at], 2)):
            place = (x + steps) % 4 * 8 + (z_pair + pairs[at]) % 4 * 2
            weights.append(block)
            places.append(place + core)
            weights.append(send(block, OTHER_CORE, freed[at]))
            places.append(place + 1 - core)
    parts = []
    for offset, result in zip(OFFSETS, results):
        parts.append(
            result
            if offset == (0, 0)
            else send(result, seq_moves(offset, back=True), axes="seq")
        )
    shard_at = jnp.stack(places).astype(jnp.int32)
    gated, tangent = project(
        weights, shard_at, parts, groups, gate_scale, gate_tangent
    )
    return (gated, tangent)


def solution(mesh):
    rows = P("dp", "seq", None)
    placed = (rows,) * 6 + (P("dp", None),) * 3
    return jax.shard_map(
        on_device,
        mesh=mesh,
        in_specs=placed,
        out_specs=(rows, rows),
        check_vma=False,
    )
```

```python
import math

import jax
import jax.numpy as jnp
from jax import lax
from jax.experimental import pallas as pl
from jax.experimental.pallas import tpu as pltpu
from jax.sharding import PartitionSpec as P

HEAD_DIM = 128
MIB = 1024 * 1024


def flat(x, z, core, y):
    dp = (x % 4) * 8 + ((z % 8) // 2) * 2 + core
    return dp * 8 + (z % 2) * 4 + y % 4


def moves(target):
    return [
        (flat(x, z, core, y), flat(*target(x, z, core, y)))
        for x in range(4)
        for z in range(8)
        for core in range(2)
        for y in range(4)
    ]


AXES = ("dp", "seq")
NEXT_X = moves(lambda x, z, core, y: (x + 1, z, core, y))
LAST_X = moves(lambda x, z, core, y: (x - 1, z, core, y))
OUTER_Z = moves(lambda x, z, core, y: (x, z + 1 if z % 2 else z - 1, core, y))
INNER_Z = moves(lambda x, z, core, y: (x, z - 1 if z % 2 else z + 1, core, y))
OTHER_CORE = moves(lambda x, z, core, y: (x, z, 1 - core, y))
PLANES = [[x * 8 + pair * 2 + core for x in range(4) for core in range(2)] for pair in range(4)]


def pack_kernel(*refs):
    ins, outs = refs[:6], refs[6:]
    pieces = outs[0].shape[0]
    width = sum(out_ref.shape[3] for out_ref in outs)
    first = 0
    for out_ref in outs:
        share = out_ref.shape[3]
        for piece in range(pieces):
            columns = slice(piece * width + first, piece * width + first + share)
            for at, ref in enumerate(ins):
                out_ref[piece, at] = ref[0, :, columns]
        first += share


def pack(arrays, pieces, shares, block=32):
    rows = arrays[0].shape[1]
    columns = arrays[0].shape[2]
    shapes = [(pieces, len(arrays), rows, share) for share in shares]
    return pl.pallas_call(
        pack_kernel,
        grid=(rows // block,),
        in_specs=[pl.BlockSpec((1, block, columns), lambda i: (0, i, 0)) for _ in arrays],
        out_specs=[
            pl.BlockSpec((pieces, len(arrays), block, share), lambda i: (0, 0, i, 0))
            for share in shares
        ],
        out_shape=[jax.ShapeDtypeStruct(shape, arrays[0].dtype) for shape in shapes],
        cost_estimate=pl.CostEstimate(
            flops=0, bytes_accessed=4 * len(arrays) * rows * columns, transcendentals=0
        ),
        name="pack",
    )(*arrays)


def dot_rows(a, b):
    return lax.dot_general(a, b, (((1,), (1,)), ((), ())), preferred_element_type=jnp.float32)


def attend_kernel(in_ref, *refs):
    out_ref = refs[-1]
    pieces, _, rows, _ = in_ref.shape
    factor = 1.0 / math.sqrt(HEAD_DIM)
    tokens = pieces * rows

    def part(at):
        return in_ref[:, at].reshape(tokens, HEAD_DIM)

    key, value = part(1), part(2)
    keys = jnp.concatenate((key, part(4)), axis=1)
    values = jnp.concatenate((value, part(5)), axis=1)
    step = 2
    for block in range(0, pieces, step):
        which = slice(block, block + step)
        query = in_ref[which, 0].reshape(step * rows, HEAD_DIM)
        query_tan = in_ref[which, 3].reshape(step * rows, HEAD_DIM)
        scores = dot_rows(query, key)
        tangent = dot_rows(jnp.concatenate((query_tan, query), axis=1), keys)
        row_max = jnp.max(scores, axis=1, keepdims=True)
        powers = jnp.exp((scores - row_max) * factor)
        product = powers * tangent
        total = jnp.sum(powers, axis=1, keepdims=True)
        product_sum = jnp.sum(product, axis=1, keepdims=True)
        both = jnp.dot(powers.astype(jnp.bfloat16), values, preferred_element_type=jnp.float32)
        third = jnp.dot(product.astype(jnp.bfloat16), value, preferred_element_type=jnp.float32)
        inverse = 1.0 / total
        attended = both[:, :HEAD_DIM] * inverse
        mean = product_sum * (inverse * factor)
        heads_tan = third * (inverse * factor) + both[:, HEAD_DIM:] * inverse - mean * attended
        out_ref[which, 0] = attended.astype(jnp.bfloat16).reshape(step, rows, HEAD_DIM)
        out_ref[which, 1] = heads_tan.astype(jnp.bfloat16).reshape(step, rows, HEAD_DIM)


def attend(received, first, width, others=None):
    pieces, count, rows, share = received.shape
    heads = share // HEAD_DIM
    tokens = rows * pieces
    kept = [] if others is None else [others]
    return pl.pallas_call(
        attend_kernel,
        grid=(heads,),
        in_specs=[pl.BlockSpec((pieces, count, rows, HEAD_DIM), lambda h: (0, 0, 0, h))]
        + [pl.BlockSpec(memory_space=pl.ANY)] * len(kept),
        out_specs=pl.BlockSpec((pieces, 2, rows, HEAD_DIM), lambda h: (0, 0, 0, h + first)),
        out_shape=jax.ShapeDtypeStruct((pieces, 2, rows, width), jnp.bfloat16),
        input_output_aliases={1: 0} if kept else {},
        compiler_params=pltpu.CompilerParams(vmem_limit_bytes=32 * MIB),
        cost_estimate=pl.CostEstimate(
            flops=heads * 12 * tokens * tokens * HEAD_DIM,
            bytes_accessed=heads * (count + 2) * tokens * HEAD_DIM * 2,
            transcendentals=heads * tokens * tokens,
        ),
        name="attend",
    )(received, *kept)


BLOCK = 512


def project_kernel(place_ref, *refs):
    x_ref, scale_ref, tan_ref, gated_ref, out_tan_ref, all_ref, held_ref, sem = refs[-8:]
    weights = refs[:-8]
    blocks, depth, _ = held_ref.shape
    height = depth // place_ref.shape[0]
    for n in range(blocks):
        at = 0
        for weight in weights:
            for first in range(0, weight.shape[0], height):
                place = pl.ds(pl.multiple_of(place_ref[at] * height, height), height)
                pltpu.make_async_copy(
                    weight.at[pl.ds(first, height), n * BLOCK : (n + 1) * BLOCK],
                    held_ref.at[n, place, :],
                    sem.at[n],
                ).start()
                at += 1
    pieces, _, rows, width = x_ref.shape
    for piece in range(pieces):
        columns = slice(piece * width, (piece + 1) * width)
        all_ref[:rows, columns] = x_ref[piece, 0]
        all_ref[rows:, columns] = x_ref[piece, 1]
    for n in range(blocks):
        pltpu.make_async_copy(held_ref.at[n], held_ref.at[n], sem.at[n]).wait()
        projected = jnp.dot(all_ref[...], held_ref[n], preferred_element_type=jnp.float32)
        primal, tangent = projected[:rows], projected[rows:]
        columns = slice(n * BLOCK, (n + 1) * BLOCK)
        scale = scale_ref[:, columns]
        gated_ref[0, :, columns] = (scale * primal).astype(jnp.bfloat16)
        out_tan_ref[0, :, columns] = (tan_ref[:, columns] * primal + scale * tangent).astype(
            jnp.bfloat16
        )


def project(weights, places, x, gate_scale, gate_tangent):
    columns = weights[0].shape[1]
    depth = sum(weight.shape[0] for weight in weights)
    rows = x.shape[2]
    out = jax.ShapeDtypeStruct((1, rows, columns), jnp.bfloat16)
    in_vmem = pl.BlockSpec(memory_space=pltpu.VMEM)
    return pl.pallas_call(
        project_kernel,
        in_specs=[pl.BlockSpec(memory_space=pltpu.SMEM)]
        + [pl.BlockSpec(memory_space=pl.ANY)] * len(weights)
        + [in_vmem] * 3,
        out_specs=[in_vmem] * 2,
        out_shape=[out, out],
        scratch_shapes=[
            pltpu.VMEM((2 * rows, depth), jnp.bfloat16),
            pltpu.VMEM((columns // BLOCK, depth, BLOCK), jnp.bfloat16),
            pltpu.SemaphoreType.DMA((columns // BLOCK,)),
        ],
        compiler_params=pltpu.CompilerParams(vmem_limit_bytes=60 * MIB),
        cost_estimate=pl.CostEstimate(
            flops=4 * rows * depth * columns,
            bytes_accessed=2 * depth * columns,
            transcendentals=0,
        ),
        name="project",
    )(places, *weights, x, gate_scale, gate_tangent)


def send(value, moves_of, *after):
    if after:
        value = lax.optimization_barrier((value,) + after)[0]
    return lax.ppermute(value, AXES, moves_of)


def gather_plane(shard):
    return lax.all_gather(shard, "dp", axis=0, tiled=True, axis_index_groups=PLANES)


def on_device(
    query_rows,
    key_rows,
    value_rows,
    query_tangent,
    key_tangent,
    value_tangent,
    out_weight,
    gate_scale,
    gate_tangent,
):
    dp, seq = lax.axis_index("dp"), lax.axis_index("seq")
    x, z_pair, core, toward = dp // 8, dp // 2 % 4, dp % 2, seq // 4 * 2 - 1
    arrays = (query_rows, key_rows, value_rows, query_tangent, key_tangent, value_tangent)

    groups = lax.axis_size("seq")
    width = query_rows.shape[2] // groups
    z = [out_weight, send(out_weight, OUTER_Z)]
    weights = [gather_plane(z[0])]
    sent = pack(arrays, groups, (HEAD_DIM, width - HEAD_DIM))
    received = lax.all_to_all(sent[0], "seq", 0, 0, tiled=True)
    z.append(send(z[1], INNER_Z, sent[0]))
    along = lax.optimization_barrier((jnp.concatenate((z[1], z[2])), received))[0]
    weights.append(gather_plane(along))
    z.append(send(z[2], OUTER_Z, received))
    before, later = send(z[3], NEXT_X), send(z[3], LAST_X)
    far = send(before, NEXT_X)
    last_sent = lax.optimization_barrier((sent[1], received))[0]
    last_received = lax.all_to_all(last_sent, "seq", 0, 0, tiled=True)
    results = attend(received, 0, width)
    last_received = lax.optimization_barrier((last_received, before, later))[0]
    results = attend(last_received, 1, width, results)
    results = lax.all_to_all(results, "seq", 0, 0, tiled=True)

    places = [s // 2 * 8 + z_pair * 2 + s % 2 for s in range(8)]
    for s in range(8):
        for pairs in (toward, -toward):
            places.append(s // 2 * 8 + (z_pair + pairs) % 4 * 2 + s % 2)
    for block, steps in ((z[3], 0), (before, -1), (later, 1), (far, 2)):
        place = (x + steps) % 4 * 8 + (z_pair + 2) % 4 * 2
        weights += [block, send(block, OTHER_CORE)]
        places += [place + core, place + 1 - core]
    gated, tangent = project(
        weights, jnp.stack(places).astype(jnp.int32), results, gate_scale, gate_tangent
    )
    return (gated, tangent)


def solution(mesh):
    rows = P("dp", "seq", None)
    placed = (rows,) * 6 + (P("dp", None),) * 3
    return jax.shard_map(
        on_device,
        mesh=mesh,
        in_specs=placed,
        out_specs=(rows, rows),
        check_vma=False,
    )
```

```python
import math

import jax
import jax.numpy as jnp
from jax import lax
from jax.experimental import pallas as pl
from jax.experimental.pallas import tpu as pltpu
from jax.sharding import PartitionSpec as P

HEAD_DIM = 128
MIB = 1024 * 1024


def flat(x, z, core, y):
    dp = (x % 4) * 8 + ((z % 8) // 2) * 2 + core
    return dp * 8 + (z % 2) * 4 + y % 4


def moves(target):
    return [
        (flat(x, z, core, y), flat(*target(x, z, core, y)))
        for x in range(4)
        for z in range(8)
        for core in range(2)
        for y in range(4)
    ]


AXES = ("dp", "seq")
NEXT_X = moves(lambda x, z, core, y: (x + 1, z, core, y))
LAST_X = moves(lambda x, z, core, y: (x - 1, z, core, y))
OUTER_Z = moves(lambda x, z, core, y: (x, z + 1 if z % 2 else z - 1, core, y))
INNER_Z = moves(lambda x, z, core, y: (x, z - 1 if z % 2 else z + 1, core, y))
OTHER_CORE = moves(lambda x, z, core, y: (x, z, 1 - core, y))


def pack_kernel(*refs):
    ins, out_ref = refs[:-1], refs[-1]
    pieces, _, _, width = out_ref.shape
    for piece in range(pieces):
        for at, ref in enumerate(ins):
            out_ref[piece, at] = ref[0, :, piece * width : (piece + 1) * width]


def pack(arrays, pieces, block=32):
    _, rows, columns = arrays[0].shape
    width = columns // pieces
    return pl.pallas_call(
        pack_kernel,
        grid=(rows // block,),
        in_specs=[pl.BlockSpec((1, block, columns), lambda i: (0, i, 0)) for _ in arrays],
        out_specs=pl.BlockSpec((pieces, len(arrays), block, width), lambda i: (0, 0, i, 0)),
        out_shape=jax.ShapeDtypeStruct((pieces, len(arrays), rows, width), arrays[0].dtype),
        cost_estimate=pl.CostEstimate(
            flops=0, bytes_accessed=4 * len(arrays) * rows * columns, transcendentals=0
        ),
        name="pack",
    )(*arrays)


def dot_rows(a, b):
    return lax.dot_general(a, b, (((1,), (1,)), ((), ())), preferred_element_type=jnp.float32)


def attend_kernel(in_ref, *refs):
    out_ref = refs[-1]
    pieces, _, rows, _ = in_ref.shape
    factor = 1.0 / math.sqrt(HEAD_DIM)
    tokens = pieces * rows

    def part(at):
        return in_ref[:, at].reshape(tokens, HEAD_DIM)

    key, value = part(1), part(2)
    keys = jnp.concatenate((key, part(4)), axis=1)
    values = jnp.concatenate((value, part(5)), axis=1)
    step = 2
    for block in range(0, pieces, step):
        which = slice(block, block + step)
        query = in_ref[which, 0].reshape(step * rows, HEAD_DIM)
        query_tan = in_ref[which, 3].reshape(step * rows, HEAD_DIM)
        scores = dot_rows(query, key)
        tangent = dot_rows(jnp.concatenate((query_tan, query), axis=1), keys)
        row_max = jnp.max(scores, axis=1, keepdims=True)
        powers = jnp.exp((scores - row_max) * factor)
        product = powers * tangent
        total = jnp.sum(powers, axis=1, keepdims=True)
        product_sum = jnp.sum(product, axis=1, keepdims=True)
        both = jnp.dot(powers.astype(jnp.bfloat16), values, preferred_element_type=jnp.float32)
        third = jnp.dot(product.astype(jnp.bfloat16), value, preferred_element_type=jnp.float32)
        inverse = 1.0 / total
        attended = both[:, :HEAD_DIM] * inverse
        mean = product_sum * (inverse * factor)
        heads_tan = third * (inverse * factor) + both[:, HEAD_DIM:] * inverse - mean * attended
        out_ref[which, 0] = attended.astype(jnp.bfloat16).reshape(step, rows, HEAD_DIM)
        out_ref[which, 1] = heads_tan.astype(jnp.bfloat16).reshape(step, rows, HEAD_DIM)


def attend(received, first, heads, others=None):
    pieces, count, rows, width = received.shape
    tokens = rows * pieces
    kept = [] if others is None else [others]
    return pl.pallas_call(
        attend_kernel,
        grid=(heads,),
        in_specs=[pl.BlockSpec((pieces, count, rows, HEAD_DIM), lambda h: (0, 0, 0, h + first))]
        + [pl.BlockSpec(memory_space=pl.ANY)] * len(kept),
        out_specs=pl.BlockSpec((pieces, 2, rows, HEAD_DIM), lambda h: (0, 0, 0, h + first)),
        out_shape=jax.ShapeDtypeStruct((pieces, 2, rows, width), jnp.bfloat16),
        input_output_aliases={1: 0} if kept else {},
        compiler_params=pltpu.CompilerParams(vmem_limit_bytes=32 * MIB),
        cost_estimate=pl.CostEstimate(
            flops=heads * 12 * tokens * tokens * HEAD_DIM,
            bytes_accessed=heads * (count + 2) * tokens * HEAD_DIM * 2,
            transcendentals=heads * tokens * tokens,
        ),
        name="attend",
    )(received, *kept)


BLOCK = 512


def project_kernel(place_ref, *refs):
    x_ref, scale_ref, tan_ref, gated_ref, out_tan_ref, all_ref, held_ref, sem = refs[-8:]
    weights = refs[:-8]
    blocks, depth, _ = held_ref.shape
    height = depth // place_ref.shape[0]
    for n in range(blocks):
        at = 0
        for weight in weights:
            for first in range(0, weight.shape[0], height):
                place = pl.ds(pl.multiple_of(place_ref[at] * height, height), height)
                pltpu.make_async_copy(
                    weight.at[pl.ds(first, height), n * BLOCK : (n + 1) * BLOCK],
                    held_ref.at[n, place, :],
                    sem.at[n],
                ).start()
                at += 1
    pieces, _, rows, width = x_ref.shape
    for piece in range(pieces):
        columns = slice(piece * width, (piece + 1) * width)
        all_ref[:rows, columns] = x_ref[piece, 0]
        all_ref[rows:, columns] = x_ref[piece, 1]
    for n in range(blocks):
        pltpu.make_async_copy(held_ref.at[n], held_ref.at[n], sem.at[n]).wait()
        projected = jnp.dot(all_ref[...], held_ref[n], preferred_element_type=jnp.float32)
        primal, tangent = projected[:rows], projected[rows:]
        columns = slice(n * BLOCK, (n + 1) * BLOCK)
        scale = scale_ref[:, columns]
        gated_ref[0, :, columns] = (scale * primal).astype(jnp.bfloat16)
        out_tan_ref[0, :, columns] = (tan_ref[:, columns] * primal + scale * tangent).astype(
            jnp.bfloat16
        )


def project(weights, places, x, gate_scale, gate_tangent):
    columns = weights[0].shape[1]
    depth = sum(weight.shape[0] for weight in weights)
    rows = x.shape[2]
    out = jax.ShapeDtypeStruct((1, rows, columns), jnp.bfloat16)
    in_vmem = pl.BlockSpec(memory_space=pltpu.VMEM)
    return pl.pallas_call(
        project_kernel,
        in_specs=[pl.BlockSpec(memory_space=pltpu.SMEM)]
        + [pl.BlockSpec(memory_space=pl.ANY)] * len(weights)
        + [in_vmem] * 3,
        out_specs=[in_vmem] * 2,
        out_shape=[out, out],
        scratch_shapes=[
            pltpu.VMEM((2 * rows, depth), jnp.bfloat16),
            pltpu.VMEM((columns // BLOCK, depth, BLOCK), jnp.bfloat16),
            pltpu.SemaphoreType.DMA((columns // BLOCK,)),
        ],
        compiler_params=pltpu.CompilerParams(vmem_limit_bytes=60 * MIB),
        cost_estimate=pl.CostEstimate(
            flops=4 * rows * depth * columns,
            bytes_accessed=2 * depth * columns,
            transcendentals=0,
        ),
        name="project",
    )(places, *weights, x, gate_scale, gate_tangent)


def send(value, moves_of, *after):
    if after:
        value = lax.optimization_barrier((value,) + after)[0]
    return lax.ppermute(value, AXES, moves_of)


def on_device(
    query_rows,
    key_rows,
    value_rows,
    query_tangent,
    key_tangent,
    value_tangent,
    out_weight,
    gate_scale,
    gate_tangent,
):
    dp, seq = lax.axis_index("dp"), lax.axis_index("seq")
    x, z_pair, core, toward = dp // 8, dp // 2 % 4, dp % 2, seq // 4 * 2 - 1
    arrays = (query_rows, key_rows, value_rows, query_tangent, key_tangent, value_tangent)

    sent = pack(arrays, lax.axis_size("seq"))
    received = lax.all_to_all(sent, "seq", 0, 0, tiled=True)

    z, before, later, far = {0: out_weight}, {}, {}, {}
    z[1] = send(z[0], OUTER_Z)
    before[0] = send(z[0], NEXT_X)
    later[0] = send(z[0], LAST_X)
    z[2] = send(z[1], INNER_Z, sent)
    far[0] = send(before[0], NEXT_X, sent)
    later[1] = send(z[1], LAST_X, later[0], sent)
    before[1] = send(z[1], NEXT_X, before[0])
    far[1] = send(later[1], LAST_X)
    z[3] = send(z[2], OUTER_Z)
    before[2] = send(z[2], NEXT_X, far[0])
    later[2] = send(z[2], LAST_X, later[1])
    far[2] = send(before[2], NEXT_X, before[1])
    later[3] = send(z[3], LAST_X, far[1])
    before[3] = send(z[3], NEXT_X, before[2])
    far[3] = send(later[3], LAST_X, later[2])

    freed = (before[1], far[1], far[2], before[3])
    weights, swapped, places = [], {}, []
    for at, pairs in enumerate((0, toward, -toward, 2)):
        for block, steps in ((z[at], 0), (before[at], -1), (later[at], 1), (far[at], 2)):
            place = (x + steps) % 4 * 8 + (z_pair + pairs) % 4 * 2
            swapped[at, steps] = send(block, OTHER_CORE, freed[at])
            weights += [block, swapped[at, steps]]
            places += [place + core, place + 1 - core]

    early = [swapped[at, steps] for at in (0, 1) for steps in (0, -1, 1, 2)]
    received = lax.optimization_barrier((received, z[3], before[2], later[2], *early))[0]
    results = attend(received, 0, 2)
    received = lax.optimization_barrier((received, far[2], later[3]))[0]
    results = attend(received, 2, 1, results)
    results = lax.all_to_all(results, "seq", 0, 0, tiled=True)

    gated, tangent = project(
        weights, jnp.stack(places).astype(jnp.int32), results, gate_scale, gate_tangent
    )
    return (gated, tangent)


def solution(mesh):
    rows = P("dp", "seq", None)
    placed = (rows,) * 6 + (P("dp", None),) * 3
    return jax.shard_map(
        on_device,
        mesh=mesh,
        in_specs=placed,
        out_specs=(rows, rows),
        check_vma=False,
    )
```

```python
import math

import jax
import jax.numpy as jnp
from jax import lax
from jax.experimental import pallas as pl
from jax.experimental.pallas import tpu as pltpu
from jax.sharding import PartitionSpec as P

HEAD_DIM = 128
MIB = 1024 * 1024


def flat(x, z, core, y):
    dp = (x % 4) * 8 + ((z % 8) // 2) * 2 + core
    return dp * 8 + (z % 2) * 4 + y % 4


def moves(target):
    return [
        (flat(x, z, core, y), flat(*target(x, z, core, y)))
        for x in range(4)
        for z in range(8)
        for core in range(2)
        for y in range(4)
    ]


AXES = ("dp", "seq")
NEXT_X = moves(lambda x, z, core, y: (x + 1, z, core, y))
LAST_X = moves(lambda x, z, core, y: (x - 1, z, core, y))
OUTER_Z = moves(lambda x, z, core, y: (x, z + 1 if z % 2 else z - 1, core, y))
THROUGH_Z = moves(lambda x, z, core, y: (x, z + 2 if z % 2 else z - 2, core, y))
OTHER_CORE = moves(lambda x, z, core, y: (x, z, 1 - core, y))


def pack_kernel(*refs):
    ins, out_ref = refs[:-1], refs[-1]
    pieces, _, _, width = out_ref.shape
    for piece in range(pieces):
        for at, ref in enumerate(ins):
            out_ref[piece, at] = ref[0, :, piece * width : (piece + 1) * width]


def pack(arrays, pieces, block=32):
    _, rows, columns = arrays[0].shape
    width = columns // pieces
    return pl.pallas_call(
        pack_kernel,
        grid=(rows // block,),
        in_specs=[pl.BlockSpec((1, block, columns), lambda i: (0, i, 0)) for _ in arrays],
        out_specs=pl.BlockSpec((pieces, len(arrays), block, width), lambda i: (0, 0, i, 0)),
        out_shape=jax.ShapeDtypeStruct((pieces, len(arrays), rows, width), arrays[0].dtype),
        cost_estimate=pl.CostEstimate(
            flops=0, bytes_accessed=4 * len(arrays) * rows * columns, transcendentals=0
        ),
        name="pack",
    )(*arrays)


def dot_rows(a, b):
    return lax.dot_general(a, b, (((1,), (1,)), ((), ())), preferred_element_type=jnp.float32)


def attend_kernel(in_ref, *refs):
    out_ref = refs[-1]
    pieces, _, rows, _ = in_ref.shape
    factor = 1.0 / math.sqrt(HEAD_DIM)
    tokens = pieces * rows

    def part(at):
        return in_ref[:, at].reshape(tokens, HEAD_DIM)

    key, value = part(1), part(2)
    keys = jnp.concatenate((key, part(4)), axis=1)
    values = jnp.concatenate((value, part(5)), axis=1)
    step = 2
    for block in range(0, pieces, step):
        which = slice(block, block + step)
        query = in_ref[which, 0].reshape(step * rows, HEAD_DIM)
        query_tan = in_ref[which, 3].reshape(step * rows, HEAD_DIM)
        scores = dot_rows(query, key)
        tangent = dot_rows(jnp.concatenate((query_tan, query), axis=1), keys)
        row_max = jnp.max(scores, axis=1, keepdims=True)
        powers = jnp.exp((scores - row_max) * factor)
        product = powers * tangent
        total = jnp.sum(powers, axis=1, keepdims=True)
        product_sum = jnp.sum(product, axis=1, keepdims=True)
        both = jnp.dot(powers.astype(jnp.bfloat16), values, preferred_element_type=jnp.float32)
        third = jnp.dot(product.astype(jnp.bfloat16), value, preferred_element_type=jnp.float32)
        inverse = 1.0 / total
        attended = both[:, :HEAD_DIM] * inverse
        mean = product_sum * (inverse * factor)
        heads_tan = third * (inverse * factor) + both[:, HEAD_DIM:] * inverse - mean * attended
        out_ref[which, 0] = attended.astype(jnp.bfloat16).reshape(step, rows, HEAD_DIM)
        out_ref[which, 1] = heads_tan.astype(jnp.bfloat16).reshape(step, rows, HEAD_DIM)


def attend(received, first, heads, others=None):
    pieces, count, rows, width = received.shape
    tokens = rows * pieces
    kept = [] if others is None else [others]
    return pl.pallas_call(
        attend_kernel,
        grid=(heads,),
        in_specs=[pl.BlockSpec((pieces, count, rows, HEAD_DIM), lambda h: (0, 0, 0, h + first))]
        + [pl.BlockSpec(memory_space=pl.ANY)] * len(kept),
        out_specs=pl.BlockSpec((pieces, 2, rows, HEAD_DIM), lambda h: (0, 0, 0, h + first)),
        out_shape=jax.ShapeDtypeStruct((pieces, 2, rows, width), jnp.bfloat16),
        input_output_aliases={1: 0} if kept else {},
        compiler_params=pltpu.CompilerParams(vmem_limit_bytes=32 * MIB),
        cost_estimate=pl.CostEstimate(
            flops=heads * 12 * tokens * tokens * HEAD_DIM,
            bytes_accessed=heads * (count + 2) * tokens * HEAD_DIM * 2,
            transcendentals=heads * tokens * tokens,
        ),
        name="attend",
    )(received, *kept)


BLOCK = 512


def project_kernel(place_ref, *refs):
    x_ref, scale_ref, tan_ref, gated_ref, out_tan_ref, all_ref, held_ref, sem = refs[-8:]
    weights = refs[:-8]
    blocks, depth, _ = held_ref.shape
    height = depth // place_ref.shape[0]
    for n in range(blocks):
        at = 0
        for weight in weights:
            for first in range(0, weight.shape[0], height):
                place = pl.ds(pl.multiple_of(place_ref[at] * height, height), height)
                pltpu.make_async_copy(
                    weight.at[pl.ds(first, height), n * BLOCK : (n + 1) * BLOCK],
                    held_ref.at[n, place, :],
                    sem.at[n],
                ).start()
                at += 1
    pieces, _, rows, width = x_ref.shape
    for piece in range(pieces):
        columns = slice(piece * width, (piece + 1) * width)
        all_ref[:rows, columns] = x_ref[piece, 0]
        all_ref[rows:, columns] = x_ref[piece, 1]
    for n in range(blocks):
        pltpu.make_async_copy(held_ref.at[n], held_ref.at[n], sem.at[n]).wait()
        projected = jnp.dot(all_ref[...], held_ref[n], preferred_element_type=jnp.float32)
        primal, tangent = projected[:rows], projected[rows:]
        columns = slice(n * BLOCK, (n + 1) * BLOCK)
        scale = scale_ref[:, columns]
        gated_ref[0, :, columns] = (scale * primal).astype(jnp.bfloat16)
        out_tan_ref[0, :, columns] = (tan_ref[:, columns] * primal + scale * tangent).astype(
            jnp.bfloat16
        )


def project(weights, places, x, gate_scale, gate_tangent):
    columns = weights[0].shape[1]
    depth = sum(weight.shape[0] for weight in weights)
    rows = x.shape[2]
    out = jax.ShapeDtypeStruct((1, rows, columns), jnp.bfloat16)
    in_vmem = pl.BlockSpec(memory_space=pltpu.VMEM)
    return pl.pallas_call(
        project_kernel,
        in_specs=[pl.BlockSpec(memory_space=pltpu.SMEM)]
        + [pl.BlockSpec(memory_space=pl.ANY)] * len(weights)
        + [in_vmem] * 3,
        out_specs=[in_vmem] * 2,
        out_shape=[out, out],
        scratch_shapes=[
            pltpu.VMEM((2 * rows, depth), jnp.bfloat16),
            pltpu.VMEM((columns // BLOCK, depth, BLOCK), jnp.bfloat16),
            pltpu.SemaphoreType.DMA((columns // BLOCK,)),
        ],
        compiler_params=pltpu.CompilerParams(vmem_limit_bytes=60 * MIB),
        cost_estimate=pl.CostEstimate(
            flops=4 * rows * depth * columns,
            bytes_accessed=2 * depth * columns,
            transcendentals=0,
        ),
        name="project",
    )(places, *weights, x, gate_scale, gate_tangent)


def send(value, moves_of, *after):
    if after:
        value = lax.optimization_barrier((value,) + after)[0]
    return lax.ppermute(value, AXES, moves_of)


def on_device(
    query_rows,
    key_rows,
    value_rows,
    query_tangent,
    key_tangent,
    value_tangent,
    out_weight,
    gate_scale,
    gate_tangent,
):
    dp, seq = lax.axis_index("dp"), lax.axis_index("seq")
    x, z_pair, core, toward = dp // 8, dp // 2 % 4, dp % 2, seq // 4 * 2 - 1
    arrays = (query_rows, key_rows, value_rows, query_tangent, key_tangent, value_tangent)

    sent = pack(arrays, lax.axis_size("seq"))
    z, before, later, far = {0: out_weight}, {}, {}, {}
    z[1] = send(z[0], THROUGH_Z)
    before[0] = send(z[0], NEXT_X)
    later[0] = send(z[0], LAST_X)
    sent = lax.optimization_barrier((sent, z[1], before[0], later[0]))[0]
    received = lax.all_to_all(sent, "seq", 0, 0, tiled=True)
    z[2] = send(z[0], OUTER_Z, z[1])
    far[0] = send(before[0], NEXT_X)
    later[1] = send(z[1], LAST_X)
    before[1] = send(z[1], NEXT_X, before[0])
    far[1] = send(later[1], LAST_X, later[0])
    z[3] = send(z[1], OUTER_Z)
    before[2] = send(z[2], NEXT_X, far[0])
    later[2] = send(z[2], LAST_X, later[1])
    far[2] = send(before[2], NEXT_X, before[1])
    later[3] = send(z[3], LAST_X, far[1])
    before[3] = send(z[3], NEXT_X, before[2])
    far[3] = send(later[3], LAST_X, later[2])

    freed = (before[1], far[1], far[2], before[3])
    weights, swapped, places = [], {}, []
    for at, pairs in enumerate((0, -toward, toward, 2)):
        for block, steps in ((z[at], 0), (before[at], -1), (later[at], 1), (far[at], 2)):
            place = (x + steps) % 4 * 8 + (z_pair + pairs) % 4 * 2
            swapped[at, steps] = send(block, OTHER_CORE, freed[at])
            weights += [block, swapped[at, steps]]
            places += [place + core, place + 1 - core]

    early = [swapped[at, steps] for at in (0, 1) for steps in (0, -1, 1, 2)]
    received = lax.optimization_barrier((received, z[3], before[2], later[2], *early))[0]
    results = attend(received, 0, 2)
    received = lax.optimization_barrier((received, far[2], later[3]))[0]
    results = attend(received, 2, 1, results)
    results = lax.all_to_all(results, "seq", 0, 0, tiled=True)

    gated, tangent = project(
        weights, jnp.stack(places).astype(jnp.int32), results, gate_scale, gate_tangent
    )
    return (gated, tangent)


def solution(mesh):
    rows = P("dp", "seq", None)
    placed = (rows,) * 6 + (P("dp", None),) * 3
    return jax.shard_map(
        on_device,
        mesh=mesh,
        in_specs=placed,
        out_specs=(rows, rows),
        check_vma=False,
    )
```

```python
import math

import jax
import jax.numpy as jnp
from jax import lax
from jax.experimental import pallas as pl
from jax.experimental.pallas import tpu as pltpu
from jax.sharding import PartitionSpec as P

HEAD_DIM = 128
MIB = 1024 * 1024


def flat(x, z, core, y):
    dp = (x % 4) * 8 + ((z % 8) // 2) * 2 + core
    return dp * 8 + (z % 2) * 4 + y % 4


def moves(target):
    return [
        (flat(x, z, core, y), flat(*target(x, z, core, y)))
        for x in range(4)
        for z in range(8)
        for core in range(2)
        for y in range(4)
    ]


AXES = ("dp", "seq")
NEXT_X = moves(lambda x, z, core, y: (x + 1, z, core, y))
LAST_X = moves(lambda x, z, core, y: (x - 1, z, core, y))
OUTER_Z = moves(lambda x, z, core, y: (x, z + 1 if z % 2 else z - 1, core, y))
THROUGH_Z = moves(lambda x, z, core, y: (x, z + 2 if z % 2 else z - 2, core, y))
OTHER_CORE = moves(lambda x, z, core, y: (x, z, 1 - core, y))


def pack_kernel(*refs):
    ins, out_ref = refs[:-1], refs[-1]
    pieces, _, _, width = out_ref.shape
    for piece in range(pieces):
        for at, ref in enumerate(ins):
            out_ref[piece, at] = ref[0, :, piece * width : (piece + 1) * width]


def pack(arrays, pieces, block=32):
    _, rows, columns = arrays[0].shape
    width = columns // pieces
    return pl.pallas_call(
        pack_kernel,
        grid=(rows // block,),
        in_specs=[pl.BlockSpec((1, block, columns), lambda i: (0, i, 0)) for _ in arrays],
        out_specs=pl.BlockSpec((pieces, len(arrays), block, width), lambda i: (0, 0, i, 0)),
        out_shape=jax.ShapeDtypeStruct((pieces, len(arrays), rows, width), arrays[0].dtype),
        cost_estimate=pl.CostEstimate(
            flops=0, bytes_accessed=4 * len(arrays) * rows * columns, transcendentals=0
        ),
        name="pack",
    )(*arrays)


def dot_rows(a, b):
    return lax.dot_general(a, b, (((1,), (1,)), ((), ())), preferred_element_type=jnp.float32)


def attend_kernel(in_ref, out_ref):
    pieces, _, rows, _ = in_ref.shape
    factor = 1.0 / math.sqrt(HEAD_DIM)
    tokens = pieces * rows

    def part(at):
        return in_ref[:, at].reshape(tokens, HEAD_DIM)

    key, value = part(1), part(2)
    keys = jnp.concatenate((key, part(4)), axis=1)
    values = jnp.concatenate((value, part(5)), axis=1)
    step = 2
    for block in range(0, pieces, step):
        which = slice(block, block + step)
        query = in_ref[which, 0].reshape(step * rows, HEAD_DIM)
        query_tan = in_ref[which, 3].reshape(step * rows, HEAD_DIM)
        scores = dot_rows(query, key)
        tangent = dot_rows(jnp.concatenate((query_tan, query), axis=1), keys)
        row_max = jnp.max(scores, axis=1, keepdims=True)
        powers = jnp.exp((scores - row_max) * factor)
        product = powers * tangent
        total = jnp.sum(powers, axis=1, keepdims=True)
        product_sum = jnp.sum(product, axis=1, keepdims=True)
        both = jnp.dot(powers.astype(jnp.bfloat16), values, preferred_element_type=jnp.float32)
        third = jnp.dot(product.astype(jnp.bfloat16), value, preferred_element_type=jnp.float32)
        inverse = 1.0 / total
        attended = both[:, :HEAD_DIM] * inverse
        mean = product_sum * (inverse * factor)
        heads_tan = third * (inverse * factor) + both[:, HEAD_DIM:] * inverse - mean * attended
        out_ref[which, 0] = attended.astype(jnp.bfloat16).reshape(step, rows, HEAD_DIM)
        out_ref[which, 1] = heads_tan.astype(jnp.bfloat16).reshape(step, rows, HEAD_DIM)


def attend(received):
    pieces, count, rows, width = received.shape
    heads = width // HEAD_DIM
    tokens = rows * pieces
    return pl.pallas_call(
        attend_kernel,
        grid=(heads,),
        in_specs=[pl.BlockSpec((pieces, count, rows, HEAD_DIM), lambda h: (0, 0, 0, h))],
        out_specs=pl.BlockSpec((pieces, 2, rows, HEAD_DIM), lambda h: (0, 0, 0, h)),
        out_shape=jax.ShapeDtypeStruct((pieces, 2, rows, width), jnp.bfloat16),
        compiler_params=pltpu.CompilerParams(vmem_limit_bytes=32 * MIB),
        cost_estimate=pl.CostEstimate(
            flops=heads * 12 * tokens * tokens * HEAD_DIM,
            bytes_accessed=(count + 2) * tokens * width * 2,
            transcendentals=heads * tokens * tokens,
        ),
        name="attend",
    )(received)


BLOCK = 512


def project_kernel(place_ref, *refs):
    x_ref, scale_ref, tan_ref, gated_ref, out_tan_ref, all_ref, held_ref, sem = refs[-8:]
    weights = refs[:-8]
    blocks, depth, _ = held_ref.shape
    height = depth // place_ref.shape[0]
    for n in range(blocks):
        at = 0
        for weight in weights:
            for first in range(0, weight.shape[0], height):
                place = pl.ds(pl.multiple_of(place_ref[at] * height, height), height)
                pltpu.make_async_copy(
                    weight.at[pl.ds(first, height), n * BLOCK : (n + 1) * BLOCK],
                    held_ref.at[n, place, :],
                    sem.at[n],
                ).start()
                at += 1
    pieces, _, rows, width = x_ref.shape
    for piece in range(pieces):
        columns = slice(piece * width, (piece + 1) * width)
        all_ref[:rows, columns] = x_ref[piece, 0]
        all_ref[rows:, columns] = x_ref[piece, 1]
    for n in range(blocks):
        pltpu.make_async_copy(held_ref.at[n], held_ref.at[n], sem.at[n]).wait()
        projected = jnp.dot(all_ref[...], held_ref[n], preferred_element_type=jnp.float32)
        primal, tangent = projected[:rows], projected[rows:]
        columns = slice(n * BLOCK, (n + 1) * BLOCK)
        scale = scale_ref[:, columns]
        gated_ref[0, :, columns] = (scale * primal).astype(jnp.bfloat16)
        out_tan_ref[0, :, columns] = (tan_ref[:, columns] * primal + scale * tangent).astype(
            jnp.bfloat16
        )


def project(weights, places, x, gate_scale, gate_tangent):
    columns = weights[0].shape[1]
    depth = sum(weight.shape[0] for weight in weights)
    rows = x.shape[2]
    out = jax.ShapeDtypeStruct((1, rows, columns), jnp.bfloat16)
    in_vmem = pl.BlockSpec(memory_space=pltpu.VMEM)
    return pl.pallas_call(
        project_kernel,
        in_specs=[pl.BlockSpec(memory_space=pltpu.SMEM)]
        + [pl.BlockSpec(memory_space=pl.ANY)] * len(weights)
        + [in_vmem] * 3,
        out_specs=[in_vmem] * 2,
        out_shape=[out, out],
        scratch_shapes=[
            pltpu.VMEM((2 * rows, depth), jnp.bfloat16),
            pltpu.VMEM((columns // BLOCK, depth, BLOCK), jnp.bfloat16),
            pltpu.SemaphoreType.DMA((columns // BLOCK,)),
        ],
        compiler_params=pltpu.CompilerParams(vmem_limit_bytes=60 * MIB),
        cost_estimate=pl.CostEstimate(
            flops=4 * rows * depth * columns,
            bytes_accessed=2 * depth * columns,
            transcendentals=0,
        ),
        name="project",
    )(places, *weights, x, gate_scale, gate_tangent)


def send(value, moves_of, *after):
    if after:
        value = lax.optimization_barrier((value,) + after)[0]
    return lax.ppermute(value, AXES, moves_of)


def on_device(
    query_rows,
    key_rows,
    value_rows,
    query_tangent,
    key_tangent,
    value_tangent,
    out_weight,
    gate_scale,
    gate_tangent,
):
    dp, seq = lax.axis_index("dp"), lax.axis_index("seq")
    x, z_pair, core, toward = dp // 8, dp // 2 % 4, dp % 2, seq // 4 * 2 - 1
    arrays = (query_rows, key_rows, value_rows, query_tangent, key_tangent, value_tangent)

    sent = pack(arrays, lax.axis_size("seq"))
    z, before, later, far = {0: out_weight}, {}, {}, {}
    z[1] = send(z[0], THROUGH_Z)
    before[0] = send(z[0], NEXT_X)
    later[0] = send(z[0], LAST_X)
    sent = lax.optimization_barrier((sent, z[1], before[0], later[0]))[0]
    received = lax.all_to_all(sent, "seq", 0, 0, tiled=True)
    z[2] = send(z[0], OUTER_Z, z[1])
    far[0] = send(before[0], NEXT_X)
    later[1] = send(z[1], LAST_X)
    before[1] = send(z[1], NEXT_X, before[0])
    far[1] = send(later[1], LAST_X, later[0])
    z[3] = send(z[1], OUTER_Z)
    before[2] = send(z[2], NEXT_X, far[0])
    later[2] = send(z[2], LAST_X, later[1])
    far[2] = send(before[2], NEXT_X, before[1])
    later[3] = send(z[3], LAST_X, far[1])
    before[3] = send(z[3], NEXT_X, before[2])
    far[3] = send(later[3], LAST_X, later[2])

    weights, swapped, places = [], {}, []
    for at, pairs in enumerate((0, -toward, toward, 2)):
        for block, steps in ((z[at], 0), (before[at], -1), (later[at], 1), (far[at], 2)):
            place = (x + steps) % 4 * 8 + (z_pair + pairs) % 4 * 2
            after = [before[1], far[1], before[2], far[2]][at]
            swapped[at, steps] = send(block, OTHER_CORE, after)
            weights += [block, swapped[at, steps]]
            places += [place + core, place + 1 - core]

    early = [swapped[at, steps] for at in (0, 1) for steps in (0, -1, 1, 2)]
    during = [swapped[2, steps] for steps in (0, -1, 1)]
    received = lax.optimization_barrier((received, z[3], before[2], later[2], *early))[0]
    results = attend(received)
    results = lax.optimization_barrier((results, far[2], later[3], *during))[0]
    results = lax.all_to_all(results, "seq", 0, 0, tiled=True)

    gated, tangent = project(
        weights, jnp.stack(places).astype(jnp.int32), results, gate_scale, gate_tangent
    )
    return (gated, tangent)


def solution(mesh):
    rows = P("dp", "seq", None)
    placed = (rows,) * 6 + (P("dp", None),) * 3
    return jax.shard_map(
        on_device,
        mesh=mesh,
        in_specs=placed,
        out_specs=(rows, rows),
        check_vma=False,
    )
```

```python
import math

import jax
import jax.numpy as jnp
from jax import lax
from jax.experimental import pallas as pl
from jax.experimental.pallas import tpu as pltpu
from jax.sharding import PartitionSpec as P

HEAD_DIM = 128
MIB = 1024 * 1024


def flat(x, z, core, y):
    dp = (x % 4) * 8 + ((z % 8) // 2) * 2 + core
    return dp * 8 + (z % 2) * 4 + y % 4


def moves(target):
    return [
        (flat(x, z, core, y), flat(*target(x, z, core, y)))
        for x in range(4)
        for z in range(8)
        for core in range(2)
        for y in range(4)
    ]


AXES = ("dp", "seq")
NEXT_X = moves(lambda x, z, core, y: (x + 1, z, core, y))
LAST_X = moves(lambda x, z, core, y: (x - 1, z, core, y))
OUTER_Z = moves(lambda x, z, core, y: (x, z + 1 if z % 2 else z - 1, core, y))
THROUGH_Z = moves(lambda x, z, core, y: (x, z + 2 if z % 2 else z - 2, core, y))
OTHER_CORE = moves(lambda x, z, core, y: (x, z, 1 - core, y))


def pack_kernel(*refs):
    ins, out_ref = refs[:-1], refs[-1]
    pieces, _, _, width = out_ref.shape
    for piece in range(pieces):
        for at, ref in enumerate(ins):
            out_ref[piece, at] = ref[0, :, piece * width : (piece + 1) * width]


def pack(arrays, pieces, block=32):
    _, rows, columns = arrays[0].shape
    width = columns // pieces
    return pl.pallas_call(
        pack_kernel,
        grid=(rows // block,),
        in_specs=[pl.BlockSpec((1, block, columns), lambda i: (0, i, 0)) for _ in arrays],
        out_specs=pl.BlockSpec((pieces, len(arrays), block, width), lambda i: (0, 0, i, 0)),
        out_shape=jax.ShapeDtypeStruct((pieces, len(arrays), rows, width), arrays[0].dtype),
        cost_estimate=pl.CostEstimate(
            flops=0, bytes_accessed=4 * len(arrays) * rows * columns, transcendentals=0
        ),
        name="pack",
    )(*arrays)


def dot_rows(a, b):
    return lax.dot_general(a, b, (((1,), (1,)), ((), ())), preferred_element_type=jnp.float32)


def attend_kernel(in_ref, out_ref):
    pieces, _, rows, _ = in_ref.shape
    factor = 1.0 / math.sqrt(HEAD_DIM)
    tokens = pieces * rows

    def part(at):
        return in_ref[:, at].reshape(tokens, HEAD_DIM)

    key, value = part(1), part(2)
    keys = jnp.concatenate((key, part(4)), axis=1)
    values = jnp.concatenate((value, part(5)), axis=1)
    step = 2
    for block in range(0, pieces, step):
        which = slice(block, block + step)
        query = in_ref[which, 0].reshape(step * rows, HEAD_DIM)
        query_tan = in_ref[which, 3].reshape(step * rows, HEAD_DIM)
        scores = dot_rows(query, key)
        tangent = dot_rows(jnp.concatenate((query_tan, query), axis=1), keys)
        row_max = jnp.max(scores, axis=1, keepdims=True)
        powers = jnp.exp((scores - row_max) * factor)
        product = powers * tangent
        total = jnp.sum(powers, axis=1, keepdims=True)
        product_sum = jnp.sum(product, axis=1, keepdims=True)
        both = jnp.dot(powers.astype(jnp.bfloat16), values, preferred_element_type=jnp.float32)
        third = jnp.dot(product.astype(jnp.bfloat16), value, preferred_element_type=jnp.float32)
        inverse = 1.0 / total
        attended = both[:, :HEAD_DIM] * inverse
        mean = product_sum * (inverse * factor)
        heads_tan = third * (inverse * factor) + both[:, HEAD_DIM:] * inverse - mean * attended
        out_ref[which, 0] = attended.astype(jnp.bfloat16).reshape(step, rows, HEAD_DIM)
        out_ref[which, 1] = heads_tan.astype(jnp.bfloat16).reshape(step, rows, HEAD_DIM)


def attend(received):
    pieces, count, rows, width = received.shape
    heads = width // HEAD_DIM
    tokens = rows * pieces
    return pl.pallas_call(
        attend_kernel,
        grid=(heads,),
        in_specs=[pl.BlockSpec((pieces, count, rows, HEAD_DIM), lambda h: (0, 0, 0, h))],
        out_specs=pl.BlockSpec((pieces, 2, rows, HEAD_DIM), lambda h: (0, 0, 0, h)),
        out_shape=jax.ShapeDtypeStruct((pieces, 2, rows, width), jnp.bfloat16),
        compiler_params=pltpu.CompilerParams(vmem_limit_bytes=32 * MIB),
        cost_estimate=pl.CostEstimate(
            flops=heads * 12 * tokens * tokens * HEAD_DIM,
            bytes_accessed=(count + 2) * tokens * width * 2,
            transcendentals=heads * tokens * tokens,
        ),
        name="attend",
    )(received)


BLOCK = 512


def project_kernel(place_ref, *refs):
    x_ref, scale_ref, tan_ref, gated_ref, out_tan_ref, all_ref, held_ref, x_sem, sem = refs[-9:]
    weights = refs[:-9]
    blocks, depth, _ = held_ref.shape
    height = depth // place_ref.shape[0]
    pieces, _, rows, width = x_ref.shape
    for piece in range(pieces):
        for which in range(2):
            pltpu.make_async_copy(
                x_ref.at[piece, which],
                all_ref.at[pl.ds(which * rows, rows), pl.ds(piece * width, width)],
                x_sem,
            ).start()
    for n in range(blocks):
        at = 0
        for weight in weights:
            for first in range(0, weight.shape[0], height):
                place = pl.ds(pl.multiple_of(place_ref[at] * height, height), height)
                pltpu.make_async_copy(
                    weight.at[pl.ds(first, height), n * BLOCK : (n + 1) * BLOCK],
                    held_ref.at[n, place, :],
                    sem.at[n],
                ).start()
                at += 1
    pltpu.make_async_copy(all_ref, all_ref, x_sem).wait()
    for n in range(blocks):
        pltpu.make_async_copy(held_ref.at[n], held_ref.at[n], sem.at[n]).wait()
        projected = jnp.dot(all_ref[...], held_ref[n], preferred_element_type=jnp.float32)
        primal, tangent = projected[:rows], projected[rows:]
        columns = slice(n * BLOCK, (n + 1) * BLOCK)
        scale = scale_ref[:, columns]
        gated_ref[0, :, columns] = (scale * primal).astype(jnp.bfloat16)
        out_tan_ref[0, :, columns] = (tan_ref[:, columns] * primal + scale * tangent).astype(
            jnp.bfloat16
        )


def project(weights, places, x, gate_scale, gate_tangent):
    columns = weights[0].shape[1]
    depth = sum(weight.shape[0] for weight in weights)
    rows = x.shape[2]
    out = jax.ShapeDtypeStruct((1, rows, columns), jnp.bfloat16)
    in_vmem = pl.BlockSpec(memory_space=pltpu.VMEM)
    return pl.pallas_call(
        project_kernel,
        in_specs=[pl.BlockSpec(memory_space=pltpu.SMEM)]
        + [pl.BlockSpec(memory_space=pl.ANY)] * (len(weights) + 1)
        + [in_vmem] * 2,
        out_specs=[in_vmem] * 2,
        out_shape=[out, out],
        scratch_shapes=[
            pltpu.VMEM((2 * rows, depth), jnp.bfloat16),
            pltpu.VMEM((columns // BLOCK, depth, BLOCK), jnp.bfloat16),
            pltpu.SemaphoreType.DMA,
            pltpu.SemaphoreType.DMA((columns // BLOCK,)),
        ],
        compiler_params=pltpu.CompilerParams(vmem_limit_bytes=60 * MIB),
        cost_estimate=pl.CostEstimate(
            flops=4 * rows * depth * columns,
            bytes_accessed=2 * depth * columns,
            transcendentals=0,
        ),
        name="project",
    )(places, *weights, x, gate_scale, gate_tangent)


def send(value, moves_of, *after):
    if after:
        value = lax.optimization_barrier((value,) + after)[0]
    return lax.ppermute(value, AXES, moves_of)


def on_device(
    query_rows,
    key_rows,
    value_rows,
    query_tangent,
    key_tangent,
    value_tangent,
    out_weight,
    gate_scale,
    gate_tangent,
):
    dp, seq = lax.axis_index("dp"), lax.axis_index("seq")
    x, z_pair, core, toward = dp // 8, dp // 2 % 4, dp % 2, seq // 4 * 2 - 1
    arrays = (query_rows, key_rows, value_rows, query_tangent, key_tangent, value_tangent)

    sent = pack(arrays, lax.axis_size("seq"))
    z, before, later, far = {0: out_weight}, {}, {}, {}
    z[1] = send(z[0], THROUGH_Z)
    before[0] = send(z[0], NEXT_X)
    later[0] = send(z[0], LAST_X)
    sent = lax.optimization_barrier((sent, z[1], before[0], later[0]))[0]
    received = lax.all_to_all(sent, "seq", 0, 0, tiled=True)
    z[2] = send(z[0], OUTER_Z, z[1])
    far[0] = send(before[0], NEXT_X)
    later[1] = send(z[1], LAST_X)
    before[1] = send(z[1], NEXT_X, before[0])
    far[1] = send(later[1], LAST_X, later[0])
    z[3] = send(z[1], OUTER_Z)
    before[2] = send(z[2], NEXT_X, far[0])
    later[2] = send(z[2], LAST_X, later[1])
    far[2] = send(before[2], NEXT_X, before[1])
    later[3] = send(z[3], LAST_X, far[1])
    before[3] = send(z[3], NEXT_X, before[2])
    far[3] = send(later[3], LAST_X, later[2])

    late = [send(block, OTHER_CORE, far[2]) for block in (far[2], z[3], later[3])]
    swapped = {(2, 2): late[0], (3, 0): late[1], (3, 1): late[2]}
    weights, places = [], []
    for at, pairs in enumerate((0, -toward, toward, 2)):
        for block, steps in ((z[at], 0), (before[at], -1), (later[at], 1), (far[at], 2)):
            place = (x + steps) % 4 * 8 + (z_pair + pairs) % 4 * 2
            after = [[before[1]], [far[1]], [before[2]], [far[2]]][at]
            if (at, steps) == (3, -1) or (at, steps) == (3, 2):
                after = late
            if (at, steps) not in swapped:
                swapped[at, steps] = send(block, OTHER_CORE, *after)
            weights += [block, swapped[at, steps]]
            places += [place + core, place + 1 - core]

    early = [swapped[at, steps] for at in (0, 1) for steps in (0, -1, 1, 2)]
    during = [swapped[2, steps] for steps in (0, -1, 1)]
    places = jnp.stack(places).astype(jnp.int32)
    received, places = lax.optimization_barrier(
        (received, places, z[3], before[2], later[2], *early)
    )[:2]
    results = attend(received)
    results = lax.optimization_barrier((results, far[2], later[3], *during))[0]
    results = lax.all_to_all(results, "seq", 0, 0, tiled=True)

    gated, tangent = project(
        weights, places, results, gate_scale, gate_tangent
    )
    return (gated, tangent)


def solution(mesh):
    rows = P("dp", "seq", None)
    placed = (rows,) * 6 + (P("dp", None),) * 3
    return jax.shard_map(
        on_device,
        mesh=mesh,
        in_specs=placed,
        out_specs=(rows, rows),
        check_vma=False,
    )
```

```python
import math

import jax
import jax.numpy as jnp
from jax import lax
from jax.experimental import pallas as pl
from jax.experimental.pallas import tpu as pltpu
from jax.sharding import PartitionSpec as P

HEAD_DIM = 128
MIB = 1024 * 1024


def flat(x, z, core, y):
    dp = (x % 4) * 8 + ((z % 8) // 2) * 2 + core
    return dp * 8 + (z % 2) * 4 + y % 4


def moves(target):
    return [
        (flat(x, z, core, y), flat(*target(x, z, core, y)))
        for x in range(4)
        for z in range(8)
        for core in range(2)
        for y in range(4)
    ]


AXES = ("dp", "seq")
NEXT_X = moves(lambda x, z, core, y: (x + 1, z, core, y))
LAST_X = moves(lambda x, z, core, y: (x - 1, z, core, y))
OUTER_Z = moves(lambda x, z, core, y: (x, z + 1 if z % 2 else z - 1, core, y))
THROUGH_Z = moves(lambda x, z, core, y: (x, z + 2 if z % 2 else z - 2, core, y))
OTHER_CORE = moves(lambda x, z, core, y: (x, z, 1 - core, y))


def pack_kernel(*refs):
    ins, out_ref = refs[:-1], refs[-1]
    pieces, _, _, width = out_ref.shape
    for piece in range(pieces):
        for at, ref in enumerate(ins):
            out_ref[piece, at] = ref[0, :, piece * width : (piece + 1) * width]


def pack(arrays, pieces, block=32):
    _, rows, columns = arrays[0].shape
    width = columns // pieces
    return pl.pallas_call(
        pack_kernel,
        grid=(rows // block,),
        in_specs=[pl.BlockSpec((1, block, columns), lambda i: (0, i, 0)) for _ in arrays],
        out_specs=pl.BlockSpec((pieces, len(arrays), block, width), lambda i: (0, 0, i, 0)),
        out_shape=jax.ShapeDtypeStruct((pieces, len(arrays), rows, width), arrays[0].dtype),
        cost_estimate=pl.CostEstimate(
            flops=0, bytes_accessed=4 * len(arrays) * rows * columns, transcendentals=0
        ),
        name="pack",
    )(*arrays)


def dot_rows(a, b):
    return lax.dot_general(a, b, (((1,), (1,)), ((), ())), preferred_element_type=jnp.float32)


def attend_kernel(in_ref, out_ref):
    pieces, _, rows, _ = in_ref.shape
    factor = 1.0 / math.sqrt(HEAD_DIM)
    tokens = pieces * rows

    def part(at):
        return in_ref[:, at].reshape(tokens, HEAD_DIM)

    key, value = part(1), part(2)
    keys = jnp.concatenate((key, part(4)), axis=1)
    values = jnp.concatenate((value, part(5)), axis=1)
    step = 2
    for block in range(0, pieces, step):
        which = slice(block, block + step)
        query = in_ref[which, 0].reshape(step * rows, HEAD_DIM)
        query_tan = in_ref[which, 3].reshape(step * rows, HEAD_DIM)
        scores = dot_rows(query, key)
        tangent = dot_rows(jnp.concatenate((query_tan, query), axis=1), keys)
        row_max = jnp.max(scores, axis=1, keepdims=True)
        powers = jnp.exp((scores - row_max) * factor)
        product = powers * tangent
        total = jnp.sum(powers, axis=1, keepdims=True)
        product_sum = jnp.sum(product, axis=1, keepdims=True)
        both = jnp.dot(powers.astype(jnp.bfloat16), values, preferred_element_type=jnp.float32)
        third = jnp.dot(product.astype(jnp.bfloat16), value, preferred_element_type=jnp.float32)
        inverse = 1.0 / total
        attended = both[:, :HEAD_DIM] * inverse
        mean = product_sum * (inverse * factor)
        heads_tan = third * (inverse * factor) + both[:, HEAD_DIM:] * inverse - mean * attended
        out_ref[which, 0] = attended.astype(jnp.bfloat16).reshape(step, rows, HEAD_DIM)
        out_ref[which, 1] = heads_tan.astype(jnp.bfloat16).reshape(step, rows, HEAD_DIM)


def attend(received):
    pieces, count, rows, width = received.shape
    heads = width // HEAD_DIM
    tokens = rows * pieces
    return pl.pallas_call(
        attend_kernel,
        grid=(heads,),
        in_specs=[pl.BlockSpec((pieces, count, rows, HEAD_DIM), lambda h: (0, 0, 0, h))],
        out_specs=pl.BlockSpec((pieces, 2, rows, HEAD_DIM), lambda h: (0, 0, 0, h)),
        out_shape=jax.ShapeDtypeStruct((pieces, 2, rows, width), jnp.bfloat16),
        compiler_params=pltpu.CompilerParams(vmem_limit_bytes=32 * MIB),
        cost_estimate=pl.CostEstimate(
            flops=heads * 12 * tokens * tokens * HEAD_DIM,
            bytes_accessed=(count + 2) * tokens * width * 2,
            transcendentals=heads * tokens * tokens,
        ),
        name="attend",
    )(received)


BLOCK = 512


def project_kernel(place_ref, *refs):
    x_ref, scale_ref, tan_ref, gated_ref, out_tan_ref, all_ref, held_ref, sem = refs[-8:]
    weights = refs[:-8]
    blocks, depth, _ = held_ref.shape
    height = depth // place_ref.shape[0]

    def fetch(n):
        at = 0
        for weight in weights:
            for first in range(0, weight.shape[0], height):
                place = pl.ds(pl.multiple_of(place_ref[at] * height, height), height)
                pltpu.make_async_copy(
                    weight.at[pl.ds(first, height), n * BLOCK : (n + 1) * BLOCK],
                    held_ref.at[n, place, :],
                    sem.at[n],
                ).start()
                at += 1

    fetch(0)
    pieces, _, rows, width = x_ref.shape
    for piece in range(pieces):
        columns = slice(piece * width, (piece + 1) * width)
        all_ref[:rows, columns] = x_ref[piece, 0]
        all_ref[rows:, columns] = x_ref[piece, 1]
    fetch(1)
    for n in range(blocks):
        pltpu.make_async_copy(held_ref.at[n], held_ref.at[n], sem.at[n]).wait()
        if n + 2 < blocks:
            fetch(n + 2)
        projected = jnp.dot(all_ref[...], held_ref[n], preferred_element_type=jnp.float32)
        primal, tangent = projected[:rows], projected[rows:]
        columns = slice(n * BLOCK, (n + 1) * BLOCK)
        scale = scale_ref[:, columns]
        gated_ref[0, :, columns] = (scale * primal).astype(jnp.bfloat16)
        out_tan_ref[0, :, columns] = (tan_ref[:, columns] * primal + scale * tangent).astype(
            jnp.bfloat16
        )


def project(weights, places, x, gate_scale, gate_tangent):
    columns = weights[0].shape[1]
    depth = sum(weight.shape[0] for weight in weights)
    rows = x.shape[2]
    out = jax.ShapeDtypeStruct((1, rows, columns), jnp.bfloat16)
    in_vmem = pl.BlockSpec(memory_space=pltpu.VMEM)
    return pl.pallas_call(
        project_kernel,
        in_specs=[pl.BlockSpec(memory_space=pltpu.SMEM)]
        + [pl.BlockSpec(memory_space=pl.ANY)] * len(weights)
        + [in_vmem] * 3,
        out_specs=[in_vmem] * 2,
        out_shape=[out, out],
        scratch_shapes=[
            pltpu.VMEM((2 * rows, depth), jnp.bfloat16),
            pltpu.VMEM((columns // BLOCK, depth, BLOCK), jnp.bfloat16),
            pltpu.SemaphoreType.DMA((columns // BLOCK,)),
        ],
        compiler_params=pltpu.CompilerParams(vmem_limit_bytes=60 * MIB),
        cost_estimate=pl.CostEstimate(
            flops=4 * rows * depth * columns,
            bytes_accessed=2 * depth * columns,
            transcendentals=0,
        ),
        name="project",
    )(places, *weights, x, gate_scale, gate_tangent)


def send(value, moves_of, *after):
    if after:
        value = lax.optimization_barrier((value,) + after)[0]
    return lax.ppermute(value, AXES, moves_of)


def on_device(
    query_rows,
    key_rows,
    value_rows,
    query_tangent,
    key_tangent,
    value_tangent,
    out_weight,
    gate_scale,
    gate_tangent,
):
    dp, seq = lax.axis_index("dp"), lax.axis_index("seq")
    x, z_pair, core, toward = dp // 8, dp // 2 % 4, dp % 2, seq // 4 * 2 - 1
    arrays = (query_rows, key_rows, value_rows, query_tangent, key_tangent, value_tangent)

    sent = pack(arrays, lax.axis_size("seq"))
    z, before, later, far = {0: out_weight}, {}, {}, {}
    z[1] = send(z[0], THROUGH_Z)
    before[0] = send(z[0], NEXT_X)
    later[0] = send(z[0], LAST_X)
    sent = lax.optimization_barrier((sent, z[1], before[0], later[0]))[0]
    received = lax.all_to_all(sent, "seq", 0, 0, tiled=True)
    z[2] = send(z[0], OUTER_Z, z[1])
    far[0] = send(before[0], NEXT_X)
    later[1] = send(z[1], LAST_X)
    before[1] = send(z[1], NEXT_X, before[0])
    far[1] = send(later[1], LAST_X, later[0])
    z[3] = send(z[1], OUTER_Z)
    before[2] = send(z[2], NEXT_X, far[0])
    later[2] = send(z[2], LAST_X, later[1])
    far[2] = send(before[2], NEXT_X, before[1])
    later[3] = send(z[3], LAST_X, far[1])
    before[3] = send(z[3], NEXT_X, before[2])
    far[3] = send(later[3], LAST_X, later[2])

    late = [send(block, OTHER_CORE, far[2]) for block in (far[2], z[3], later[3])]
    swapped = {(2, 2): late[0], (3, 0): late[1], (3, 1): late[2]}
    weights, places = [], []
    for at, pairs in enumerate((0, -toward, toward, 2)):
        for block, steps in ((z[at], 0), (before[at], -1), (later[at], 1), (far[at], 2)):
            place = (x + steps) % 4 * 8 + (z_pair + pairs) % 4 * 2
            after = [[before[1]], [far[1]], [before[2]], [far[2]]][at]
            if (at, steps) == (3, -1) or (at, steps) == (3, 2):
                after = late
            if (at, steps) not in swapped:
                swapped[at, steps] = send(block, OTHER_CORE, *after)
            weights += [block, swapped[at, steps]]
            places += [place + core, place + 1 - core]

    early = [swapped[at, steps] for at in (0, 1) for steps in (0, -1, 1, 2)]
    during = [swapped[2, steps] for steps in (0, -1, 1)]
    places = jnp.stack(places).astype(jnp.int32)
    received, places = lax.optimization_barrier(
        (received, places, z[3], before[2], later[2], *early)
    )[:2]
    results = attend(received)
    results = lax.optimization_barrier((results, far[2], later[3], *during))[0]
    results = lax.all_to_all(results, "seq", 0, 0, tiled=True)

    gated, tangent = project(
        weights, places, results, gate_scale, gate_tangent
    )
    return (gated, tangent)


def solution(mesh):
    rows = P("dp", "seq", None)
    placed = (rows,) * 6 + (P("dp", None),) * 3
    return jax.shard_map(
        on_device,
        mesh=mesh,
        in_specs=placed,
        out_specs=(rows, rows),
        check_vma=False,
    )
```
